128 devices in a mesh: dp: 64 (over z, y, x_hi, core), tower: 2 (over x_lo).
Axes of the slice: x: 4 (x_hi: 2, x_lo: 2; x = x_hi * 2 + x_lo), y: 4, z: 4, core: 2. Of those that a mesh axis runs over, the one named last changes fastest.
Arguments:
- img_feats: bfloat16 [8192, 1152], P('dp'), may hold values from -8 to 8
- txt_feats: bfloat16 [8192, 1152], P('dp'), may hold values from -8 to 8
- img_proj: bfloat16 [1152, 1152], P(None, 'tower'), may hold values from -1 to 1
- txt_proj: bfloat16 [1152, 1152], P(None, 'tower'), may hold values from -1 to 1
Outputs:
- img_proj_grad: float32 [1152, 1152], P('dp', 'tower')
- txt_proj_grad: float32 [1152, 1152], P('dp', 'tower')
The draws below stay inside these ranges and needn't reach their ends.
All inputs are finite; a program needn't handle non-finite values.
Results may differ from the reference program's by a relative error of at most 0.004.
Values may be sent and summed in bfloat16 or wider, within the bound.
No kernel may reach another device: no remote copies, remote signals or barrier semaphores. Data moves between devices by JAX's collectives and lax.ppermute only.
A program may use at most 64 MiB of HBM per device.

```python
import math
import jax
import jax.numpy as jnp
from jax import lax

D = 1152
EMB = 1152
ROWS_DEV = 128
BATCH = 8192


def shared_latent(key, lower_end, upper_end):
    subkeys = jax.random.split(key, 4)
    groups = max(BATCH // 16, 1)
    labels = jax.random.randint(subkeys[0], (BATCH,), 0, groups)
    centers = jax.random.normal(subkeys[1], (groups, D), jnp.float32)
    member = jax.random.normal(subkeys[2], (BATCH, D), jnp.float32)
    strength = jax.random.uniform(subkeys[3], (BATCH, 1), jnp.float32, lower_end, upper_end)
    return strength * jnp.take(centers, labels, axis=0) + 0.6 * member


def shared_head(key):
    return jax.random.normal(jax.random.fold_in(key, 101), (D, EMB), jnp.float32)


def draw_img_feats(key, part):
    latent = shared_latent(key, 0.4, 1.6)
    key = jax.random.fold_in(key, 3)
    noise = 0.35 * jax.random.normal(key, (BATCH, D), jnp.float32)
    return jnp.clip(latent + noise, -8.0, 8.0).astype(jnp.bfloat16)


def draw_txt_feats(key, part):
    latent = shared_latent(key, 0.4, 1.6)
    key = jax.random.fold_in(key, 4)
    noise = 0.35 * jax.random.normal(key, (BATCH, D), jnp.float32)
    return jnp.clip(latent + noise, -8.0, 8.0).astype(jnp.bfloat16)


def draw_img_proj(key, part):
    common = shared_head(key)
    key = jax.random.fold_in(key, 5)
    own = jax.random.normal(key, (D, EMB), jnp.float32)
    mixed = (common + 0.35 * own) / math.sqrt(1.1225 * D)
    return jnp.clip(mixed, -1.0, 1.0).astype(jnp.bfloat16)


def draw_txt_proj(key, part):
    common = shared_head(key)
    key = jax.random.fold_in(key, 6)
    own = jax.random.normal(key, (D, EMB), jnp.float32)
    mixed = (common + 0.35 * own) / math.sqrt(1.1225 * D)
    return jnp.clip(mixed, -1.0, 1.0).astype(jnp.bfloat16)


def setup_inputs(seed: int = 0) -> dict:
    splits = jax.random.split(jax.random.key(seed), 5)
    return {
        "img_feats": draw_img_feats(jax.random.fold_in(splits[4], 71), 0),
        "txt_feats": draw_txt_feats(jax.random.fold_in(splits[4], 71), 0),
        "img_proj": draw_img_proj(jax.random.fold_in(splits[4], 71), 0),
        "txt_proj": draw_txt_proj(jax.random.fold_in(splits[4], 71), 0),
    }


logit_scale = 10.0
logit_bias = -10.0
norm_eps = 1e-06

def embed(feats, proj):
    raw = jnp.dot(feats, proj, preferred_element_type=jnp.float32).astype(jnp.bfloat16)
    wide = raw.astype(jnp.float32)
    norm = jnp.sqrt(lax.optimization_barrier(jnp.sum(wide * wide, axis=1, keepdims=True)) + norm_eps)
    unit = wide / norm
    return (unit.astype(jnp.bfloat16), unit, norm)

def pair_coef(block_img, block_txt, positive):
    logits = logit_scale * jnp.dot(block_img, block_txt.T, preferred_element_type=jnp.float32) + logit_bias
    label = 2.0 * positive - 1.0
    return (-logit_scale * label * jax.nn.sigmoid(-label * logits)).astype(jnp.bfloat16)

def feat_grad(feats, unit, norm, direction):
    inner = lax.optimization_barrier(jnp.sum(unit * direction, axis=1, keepdims=True))
    raw_grad = ((direction - unit * inner) / norm).astype(jnp.bfloat16)
    return jnp.dot(feats.T, raw_grad, preferred_element_type=jnp.float32)

def reference(img_feats, txt_feats, img_proj, txt_proj):
    img_emb, img_unit, img_norm = embed(img_feats, img_proj)
    txt_emb, txt_unit, txt_norm = embed(txt_feats, txt_proj)
    blocks = BATCH // ROWS_DEV
    img_blocks = img_emb.reshape(blocks, ROWS_DEV, EMB)
    columns = jnp.arange(BATCH, dtype=jnp.int32)
    local_rows = jnp.arange(ROWS_DEV, dtype=jnp.int32)

    def step(txt_dir, inputs):
        index, block = inputs
        rows = index * ROWS_DEV + local_rows
        positive = (rows[:, None] == columns[None, :]).astype(jnp.float32)
        coef = pair_coef(block, txt_emb, positive)
        img_dir_block = jnp.dot(coef, txt_emb, preferred_element_type=jnp.float32)
        txt_dir = txt_dir + jnp.dot(coef.T, block, preferred_element_type=jnp.float32)
        return (txt_dir, img_dir_block)
    txt_dir, img_dir = lax.scan(step, jnp.zeros((BATCH, EMB), jnp.float32), (jnp.arange(blocks, dtype=jnp.int32), img_blocks))
    img_dir = img_dir.reshape(BATCH, EMB)
    img_proj_grad = feat_grad(img_feats, img_unit, img_norm, img_dir)
    txt_proj_grad = feat_grad(txt_feats, txt_unit, txt_norm, txt_dir)
    return (img_proj_grad, txt_proj_grad)
```

```python
import functools

import jax
import jax.numpy as jnp
from jax import lax
from jax.experimental import pallas as pl
from jax.experimental.pallas import tpu as pltpu
from jax.sharding import PartitionSpec as P

logit_scale = 10.0
logit_bias = -10.0
norm_eps = 1e-06
AXES = ("dp", "tower")
RING = 4
UNITS = 8
MIB = 1 << 20


def device(z, y, x, core):
    return (((z % 4 * 4 + y % 4) * 2 + x // 2) * 2 + core) * 2 + x % 2


def chips():
    return [(z, y, x) for z in range(RING) for y in range(RING) for x in range(RING)]


def swap_cores():
    return [(device(*chip, core), device(*chip, 1 - core)) for chip in chips() for core in range(2)]


def swap_towers():
    return [
        (device(z, y, x, core), device(z, y, x ^ 1, core)) for z, y, x in chips() for core in range(2)
    ]


def gather_pairs(turn, flip):
    pairs = []
    for z, y, x in chips():
        pairs.append((device(z + turn, y, x ^ 1 if flip else x, 0), device(z, y, x, 0)))
        pairs.append((device(z, y + turn, 3 - x if flip else x, 1), device(z, y, x, 1)))
    return pairs


def reduce_pairs(turn, flip):
    return [
        (device(z, y, x, core), device(z + turn, y, x ^ 1 if flip else x, core))
        for z, y, x in chips()
        for core in range(2)
    ]


def reduce_groups():
    return [
        [device(z, y, 2 * hi + lo, core) for y in range(RING) for hi in range(2)]
        for z in range(RING)
        for lo in range(2)
        for core in range(2)
    ]


OFFSETS = [(turn, flip) for flip in range(2) for turn in range(RING)]


def embed_kernel(*refs):
    units, (own_ref, far_ref), (emb_ref, raw_ref, norm_ref), head = (
        refs[:UNITS], refs[UNITS : UNITS + 2], refs[UNITS + 2 : UNITS + 5], refs[UNITS + 5]
    )
    width = own_ref.shape[1]
    rows = units[0].shape[0]
    head[:, :width] = own_ref[...]
    head[:, width:] = far_ref[...]
    for i in range(0, UNITS, 2):
        feats = jnp.concatenate([units[i][...], units[i + 1][...]], axis=0)
        raw = jnp.dot(feats, head[...], preferred_element_type=jnp.float32).astype(jnp.bfloat16)
        wide = raw.astype(jnp.float32)
        norm = jnp.sqrt(jnp.sum(wide * wide, axis=1, keepdims=True) + norm_eps)
        here = pl.ds(i * rows, 2 * rows)
        emb_ref[here, :] = (wide / norm).astype(jnp.bfloat16)
        raw_ref[here, :] = raw
        norm_ref[here, :] = norm


def score_kernel(*refs):
    (where_ref, emb_ref, far_ref, raw_ref, norm_ref), units, pieces, (flipped, grads, coefs) = (
        refs[:5], refs[5 : 5 + UNITS], refs[5 + UNITS : 5 + 2 * UNITS], refs[5 + 2 * UNITS :]
    )
    rows = units[0].shape[0]
    tile = 2 * rows
    for i in range(UNITS):
        flipped[:, i * rows : (i + 1) * rows] = units[i][...].T

    def step(i, carry):
        here = pl.ds(pl.multiple_of(i * tile, tile), tile)
        logits = (
            logit_scale
            * lax.dot_general(
                emb_ref[here, :], far_ref[...], (((1,), (1,)), ((), ())), preferred_element_type=jnp.float32
            )
            + logit_bias
        )
        coefs[...] = (logit_scale / (1.0 + jnp.exp(-logits))).astype(jnp.bfloat16)

        @pl.when(i == 0)
        def _():
            block = logits[:rows, :rows]
            match = lax.broadcasted_iota(jnp.int32, (rows, rows), 0) == lax.broadcasted_iota(
                jnp.int32, (rows, rows), 1
            )
            value = logit_scale / (1.0 + jnp.exp(jnp.where(match, block, -block)))
            coefs[:rows, :rows] = jnp.where(match, -value, value).astype(jnp.bfloat16)

        direction = jnp.dot(coefs[...], far_ref[...], preferred_element_type=jnp.float32)
        norm = norm_ref[here, :]
        unit = raw_ref[here, :].astype(jnp.float32) / norm
        inner = jnp.sum(unit * direction, axis=1, keepdims=True)
        grads[here, :] = ((direction - unit * inner) / norm).astype(jnp.bfloat16)
        return carry

    lax.fori_loop(0, UNITS // 2, step, 0)
    depth, width = pieces[0].shape
    for k, (turn, flip) in enumerate(OFFSETS):
        ring = lax.rem(where_ref[0] + turn, RING)
        feats = flipped[pl.ds(pl.multiple_of(ring * depth, 32), depth), :]
        pieces[k][...] = jnp.dot(
            feats, grads[:, flip * width : (flip + 1) * width], preferred_element_type=jnp.float32
        ).astype(jnp.bfloat16)


def sum_kernel(*refs):
    total = refs[0][...].astype(jnp.float32)
    for ref in refs[1:-1]:
        total += ref[...].astype(jnp.float32)
    out_ref = refs[-1]
    part = out_ref.shape[1]
    for j in range(UNITS):
        out_ref[j] = total[j * part : (j + 1) * part, :]


def local(img_feats, txt_feats, img_proj, txt_proj):
    rows, depth = img_feats.shape
    width = img_proj.shape[1]
    batch = UNITS * rows
    dp_id = lax.axis_index("dp")
    tower_id = lax.axis_index("tower")
    core = lax.rem(dp_id, 2)
    high = lax.rem(lax.div(dp_id, 2), 2)
    is_img = core == 0

    head = jnp.where(is_img, img_proj, txt_proj)
    head_far = lax.ppermute(head, AXES, swap_towers())
    mine = jnp.where(is_img, img_feats, txt_feats)
    other = lax.ppermute(jnp.where(is_img, txt_feats, img_feats), AXES, swap_cores())
    pick = (high == tower_id).astype(jnp.int32)
    unit = jnp.where(pick == core, mine, other)
    units = [unit] + [lax.ppermute(unit, AXES, gather_pairs(*offset)) for offset in OFFSETS[1:]]

    emb, raw, norm = pl.pallas_call(
        embed_kernel,
        out_shape=(
            jax.ShapeDtypeStruct((batch, 2 * width), jnp.bfloat16),
            jax.ShapeDtypeStruct((batch, 2 * width), jnp.bfloat16),
            jax.ShapeDtypeStruct((batch, 1), jnp.float32),
        ),
        scratch_shapes=[pltpu.VMEM((depth, 2 * width), jnp.bfloat16)],
        compiler_params=pltpu.CompilerParams(vmem_limit_bytes=40 * MIB),
        cost_estimate=pl.CostEstimate(
            flops=4 * batch * depth * width, bytes_accessed=10 * MIB, transcendentals=0
        ),
        name="embed",
    )(*units, head, head_far)
    emb_far = lax.ppermute(emb, AXES, swap_cores())

    place = lax.div(dp_id, 16).astype(jnp.int32).reshape(1)
    part = depth // RING
    vmem = pl.BlockSpec(memory_space=pltpu.VMEM)
    pieces = pl.pallas_call(
        score_kernel,
        out_shape=[jax.ShapeDtypeStruct((part, width), jnp.bfloat16)] * UNITS,
        in_specs=[pl.BlockSpec(memory_space=pltpu.SMEM)] + [vmem] * (4 + UNITS),
        out_specs=[vmem] * UNITS,
        scratch_shapes=[
            pltpu.VMEM((depth, batch), jnp.bfloat16),
            pltpu.VMEM((batch, 2 * width), jnp.bfloat16),
            pltpu.VMEM((2 * rows, batch), jnp.bfloat16),
        ],
        compiler_params=pltpu.CompilerParams(vmem_limit_bytes=48 * MIB),
        cost_estimate=pl.CostEstimate(
            flops=8 * batch * batch * width + 4 * batch * depth * width,
            bytes_accessed=14 * MIB,
            transcendentals=batch * batch,
        ),
        name="score",
    )(place, emb, emb_far, raw, norm, *units)
    terms = [pieces[0]] + [
        lax.ppermute(piece, AXES, reduce_pairs(*offset)) for piece, offset in zip(pieces[1:], OFFSETS[1:])
    ]
    sums = pl.pallas_call(
        sum_kernel,
        out_shape=jax.ShapeDtypeStruct((UNITS, part // UNITS, width), jnp.float32),
        compiler_params=pltpu.CompilerParams(vmem_limit_bytes=24 * MIB),
        name="sum_pieces",
    )(*terms)
    swapped = lax.all_to_all(
        sums, AXES, 0, 0, axis_index_groups=reduce_groups(), tiled=True
    )
    total = jnp.sum(swapped, axis=0)
    half = total.shape[0] // 2
    low, top = total[:half], total[half:]
    keep = jnp.where(is_img, low, top)
    got = lax.ppermute(jnp.where(is_img, top, low), AXES, swap_cores())
    return (jnp.where(is_img, keep, got), jnp.where(is_img, got, keep))


def solution(mesh):
    return jax.shard_map(
        local,
        mesh=mesh,
        in_specs=(P("dp", None), P("dp", None), P(None, "tower"), P(None, "tower")),
        out_specs=(P("dp", "tower"), P("dp", "tower")),
        check_vma=False,
    )
```

```python
import jax
import jax.numpy as jnp
from jax import lax
from jax.experimental import pallas as pl
from jax.experimental.pallas import tpu as pltpu
from jax.sharding import PartitionSpec as P

logit_scale = 10.0
logit_bias = -10.0
norm_eps = 1e-06
AXES = ("dp", "tower")
RING = 4
MIB = 1 << 20
F32, BF16 = jnp.float32, jnp.bfloat16


def device(z, y, x, core):
    return (((z % 4 * 4 + y % 4) * 2 + x // 2) * 2 + core) * 2 + x % 2


CHIPS = [(z, y, x) for z in range(RING) for y in range(RING) for x in range(RING)]
CORES_SWAP = [(device(*chip, core), device(*chip, 1 - core)) for chip in CHIPS for core in range(2)]
TOWERS_SWAP = [(device(z, y, x, core), device(z, y, x ^ 1, core)) for z, y, x in CHIPS for core in range(2)]


def gather_pairs(turn):
    source = (0, 2, 1, 3)
    pairs = []
    for z, y, x in CHIPS:
        pairs.append((device(z + turn, y, x, 0), device(z, y, x, 0)))
        pairs.append((device(z, y + turn, source[x], 1), device(z, y, x, 1)))
    return pairs


def reduce_pairs(turn, flip):
    pairs = []
    for z, y, x in CHIPS:
        pairs.append((device(z, y, x, 0), device(z + turn, y, x ^ flip, 0)))
        pairs.append((device(z, y, x, 1), device(z, y + turn, x ^ (2 * flip), 1)))
    return pairs


REDUCE_GROUPS = [
    [device(z, y, 2 * high + tower, 0) for y in range(RING) for high in range(2)]
    for z in range(RING)
    for tower in range(2)
] + [
    [device(z, y, 2 * high + tower, 1) for z in range(RING) for tower in range(2)]
    for y in range(RING)
    for high in range(2)
]


def position():
    dp = lax.axis_index("dp")
    return (
        lax.div(dp, 16),
        lax.rem(lax.div(dp, 4), 4),
        lax.rem(lax.div(dp, 2), 2),
        lax.rem(dp, 2),
        lax.axis_index("tower"),
    )


def vmem():
    return pl.BlockSpec(memory_space=pltpu.VMEM)


def pick_kernel(img_feats, txt_feats, img_proj, txt_proj, mine, give, top, bottom, head, sems):
    core = position()[3]

    def copies(feats, other, proj):
        return [
            pltpu.make_async_copy(proj, head, sems.at[0]),
            pltpu.make_async_copy(other, give, sems.at[1]),
            pltpu.make_async_copy(feats, mine, sems.at[2]),
        ]

    @pl.when(core == 0)
    def _():
        for copy in copies(img_feats, txt_feats, img_proj):
            copy.start()

    @pl.when(core == 1)
    def _():
        for copy in copies(txt_feats, img_feats, txt_proj):
            copy.start()

    for copy in copies(img_feats, txt_feats, img_proj):
        copy.wait()
    part, width = top.shape[0], head.shape[1]
    top[:, :width] = head[:part, :]
    bottom[:, :width] = head[part : 2 * part, :]
    top[:, width:] = head[2 * part : 3 * part, :]
    bottom[:, width:] = head[3 * part :, :]


def flip_rows(feats, flip_ref, lane):
    z, y, high, core, _ = position()
    part = flip_ref.shape[2] // RING
    turned = feats.T

    def store(own, ring_first):
        for block in range(2 * RING * RING):
            first, second, side = block // 8, block // 2 % 4, block % 2
            ring, other = (first, second) if ring_first else (second, first)
            turn = lax.rem(ring - own + RING, RING)
            flip_ref[turn, lax.rem(side + high, 2), pl.ds(other * part, part), pl.ds(lane, feats.shape[0])] = (
                turned[block * part : (block + 1) * part, :]
            )

    @pl.when(core == 0)
    def _():
        store(z, True)

    @pl.when(core == 1)
    def _():
        store(y, False)


def embed_rows(feats, head, here, emb_ref, raw_ref):
    raw = jnp.dot(feats, head, preferred_element_type=F32).astype(BF16)
    wide = raw.astype(F32)
    norm = jnp.sqrt(jnp.sum(wide * wide, axis=1, keepdims=True) + norm_eps)
    emb_ref[here, :] = (wide / norm).astype(BF16)
    raw_ref[here, :] = raw


def embed_first_kernel(top, bottom, far_top, far_bottom, one, two, emb_ref, raw_ref, flip_ref, head_ref):
    part, width = top.shape[0], top.shape[1] // 2
    for column, (upper, lower) in ((0, (top, bottom)), (width, (far_top, far_bottom))):
        head_ref[0:part, column : column + width] = upper[:, :width]
        head_ref[part : 2 * part, column : column + width] = lower[:, :width]
        head_ref[2 * part : 3 * part, column : column + width] = upper[:, width:]
        head_ref[3 * part :, column : column + width] = lower[:, width:]
    rows = one.shape[0]
    for i, unit in enumerate((one, two)):
        embed_rows(unit[...], head_ref[...], pl.ds(i * rows, rows), emb_ref, raw_ref)
        flip_rows(unit[...], flip_ref, i * rows)


def embed_second_kernel(head_ref, one, two, emb_ref, raw_ref, flip_ref):
    rows = one.shape[0]
    for i, unit in enumerate((one, two)):
        embed_rows(unit[...], head_ref[...], pl.ds(i * rows, rows), emb_ref, raw_ref)
        flip_rows(unit[...], flip_ref, i * rows)


def score_kernel(emb_a, emb_b, far_a, far_b, raw_a, raw_b, grad_a, grad_b, turned_a, turned_b):
    _, _, high, _, tower = position()
    turned_a[...] = far_a[...].T
    turned_b[...] = far_b[...].T
    rows = emb_a.shape[0] // 2

    def coef(logits):
        return (logit_scale / (1.0 + jnp.exp(-(logit_scale * logits + logit_bias)))).astype(BF16)

    for emb, raw, grad, i in ((emb_a, raw_a, grad_a, 0), (emb_a, raw_a, grad_a, 1), (emb_b, raw_b, grad_b, 0), (emb_b, raw_b, grad_b, 1)):
        here = pl.ds(i * rows, rows)
        own = emb[here, :]
        coef_a = coef(jnp.dot(own, turned_a[...], preferred_element_type=F32))
        logits_b = jnp.dot(own, turned_b[...], preferred_element_type=F32)
        if emb is emb_b and i == 0:
            row = lax.broadcasted_iota(jnp.int32, (rows, rows), 0)
            column = lax.broadcasted_iota(jnp.int32, (rows, rows), 1)
            match = (jnp.abs(row - column) == rows // 2) & (high == tower)
            logits = logit_scale * logits_b[:, :rows] + logit_bias
            value = logit_scale / (1.0 + jnp.exp(jnp.where(match, logits, -logits)))
            coef_b = jnp.concatenate(
                [jnp.where(match, -value, value).astype(BF16), coef(logits_b[:, rows:])], axis=1
            )
        else:
            coef_b = coef(logits_b)
        direction = jnp.dot(coef_a, far_a[...], preferred_element_type=F32) + jnp.dot(
            coef_b, far_b[...], preferred_element_type=F32
        )
        wide = raw[here, :].astype(F32)
        norm = jnp.sqrt(jnp.sum(wide * wide, axis=1, keepdims=True) + norm_eps)
        unit = wide / norm
        inner = jnp.sum(unit * direction, axis=1, keepdims=True)
        grad[here, :] = ((direction - unit * inner) / norm).astype(BF16)


def terms_kernel(turns, flip_a, flip_b, grad_a, grad_b, *pieces):
    core = position()[3]
    for k, turn in enumerate(turns):
        half, rows = flip_a.shape[2], grad_a.shape[0]
        width = grad_a.shape[1] // 2
        term = jnp.dot(
            flip_a[turn].reshape(2 * half, rows), grad_a[...], preferred_element_type=F32
        ) + jnp.dot(flip_b[turn].reshape(2 * half, rows), grad_b[...], preferred_element_type=F32)
        term = term.astype(BF16)
        straight, crossed = pieces[2 * k], pieces[2 * k + 1]
        straight[:, :width] = term[:half, :width]
        crossed[:, width:] = term[half:, width:]

        @pl.when(core == 0)
        def _():
            straight[:, width:] = term[half:, :width]
            crossed[:, :width] = term[:half, width:]

        @pl.when(core == 1)
        def _():
            straight[:, width:] = term[:half, width:]
            crossed[:, :width] = term[half:, :width]


def sum_kernel(*refs):
    _, _, high, core, tower = position()
    out_ref = refs[-1]
    total = refs[0][...].astype(F32)
    for ref in refs[1:-1]:
        total += ref[...].astype(F32)
    total = total.astype(out_ref.dtype)
    twist = jnp.where(core == 0, high, tower)
    part, width = out_ref.shape[1], out_ref.shape[2] // 2
    for j in range(RING):
        for side in range(2):
            slot = 2 * j + lax.rem(side + twist, 2)
            columns = slice(side * width, (side + 1) * width)
            out_ref[slot, :, :width] = total[2 * j * part : (2 * j + 1) * part, columns]
            out_ref[slot, :, width:] = total[(2 * j + 1) * part : (2 * j + 2) * part, columns]


def kernel_call(body, name, shapes, operands, scratch=(), flops=0, exps=0, specs=None, limit=40):
    shapes = [jax.ShapeDtypeStruct(*shape) for shape in shapes]
    touched = sum(a.size * a.dtype.itemsize for a in (*shapes, *operands))
    return pl.pallas_call(
        body,
        out_shape=shapes,
        in_specs=[vmem()] * len(operands) if specs is None else specs,
        out_specs=[vmem()] * len(shapes),
        scratch_shapes=list(scratch),
        compiler_params=pltpu.CompilerParams(vmem_limit_bytes=limit * MIB),
        cost_estimate=pl.CostEstimate(flops=flops, bytes_accessed=touched, transcendentals=exps),
        name=name,
    )(*operands)


def local(img_feats, txt_feats, img_proj, txt_proj):
    rows, depth = img_feats.shape
    width = img_proj.shape[1]
    full = 2 * width
    unit = 2 * rows
    pair = 2 * unit
    part = depth // (2 * RING * RING)

    def swap(value):
        return lax.ppermute(value, AXES, CORES_SWAP)

    mine, give, top, bottom = kernel_call(
        pick_kernel,
        "pick",
        [((rows, depth), BF16)] * 2 + [((depth // 4, full), BF16)] * 2,
        (img_feats, txt_feats, img_proj, txt_proj),
        scratch=(pltpu.VMEM((depth, width), BF16), pltpu.SemaphoreType.DMA((3,))),
        specs=[pl.BlockSpec(memory_space=pl.ANY)] * 4,
    )
    far_top = lax.ppermute(top, AXES, TOWERS_SWAP)
    far_bottom = lax.ppermute(bottom, AXES, TOWERS_SWAP)
    own = jnp.concatenate([mine, swap(give)], axis=0)
    units = [lax.ppermute(own, AXES, gather_pairs(turn)) for turn in range(RING)]

    flips = ((RING, 2, RING * part, pair), BF16)
    block = ((pair, full), BF16)
    work = 2 * pair * depth * full
    emb_a, raw_a, flip_a, head = kernel_call(
        embed_first_kernel,
        "embed_first",
        [block, block, flips, ((depth, full), BF16)],
        (top, bottom, far_top, far_bottom, units[1], units[3]),
        flops=work,
    )
    far_a = swap(emb_a)
    emb_b, raw_b, flip_b = kernel_call(
        embed_second_kernel, "embed_second", [block, block, flips], (head, units[0], units[2]), flops=work
    )
    far_b = swap(emb_b)
    grad_a, grad_b = kernel_call(
        score_kernel,
        "score",
        [block, block],
        (emb_a, emb_b, far_a, far_b, raw_a, raw_b),
        scratch=[pltpu.VMEM((full, pair), BF16)] * 2,
        flops=16 * pair * pair * full,
        exps=4 * pair * pair,
    )

    def terms(name, turns):
        return kernel_call(
            lambda *refs: terms_kernel(turns, *refs),
            name,
            [((RING * part, full), BF16)] * (2 * len(turns)),
            (flip_a, flip_b, grad_a, grad_b),
            flops=len(turns) * work // 2,
        )

    def send(pieces, turns):
        return [
            lax.ppermute(pieces[2 * k + flip], AXES, reduce_pairs(turn, flip)) if turn or flip else pieces[0]
            for k, turn in enumerate(turns)
            for flip in range(2)
        ]

    first = send(terms("terms_first", (1, 3)), (1, 3))
    second = send(terms("terms_second", (0, 2)), (0, 2))
    (sums,) = kernel_call(
        sum_kernel, "sum_terms", [((2 * RING, part // 2, full), BF16)], (*first, *second)
    )
    swapped = lax.all_to_all(sums, AXES, 0, 0, axis_index_groups=REDUCE_GROUPS, tiled=True)
    total = jnp.sum(swapped.astype(F32), axis=0)
    is_img = position()[3] == 0
    low, high = total[:, :width], total[:, width:]
    keep = jnp.where(is_img, low, high)
    got = swap(jnp.where(is_img, high, low))
    return (jnp.where(is_img, keep, got), jnp.where(is_img, got, keep))


def solution(mesh):
    return jax.shard_map(
        local,
        mesh=mesh,
        in_specs=(P("dp", None), P("dp", None), P(None, "tower"), P(None, "tower")),
        out_specs=(P("dp", "tower"), P("dp", "tower")),
        check_vma=False,
    )
```

```python
import jax
import jax.numpy as jnp
from jax import lax
from jax.experimental import pallas as pl
from jax.experimental.pallas import tpu as pltpu
from jax.sharding import PartitionSpec as P

logit_scale = 10.0
logit_bias = -10.0
norm_eps = 1e-06
AXES = ("dp", "tower")
RING = 4
MIB = 1 << 20
F32, BF16 = jnp.float32, jnp.bfloat16


def device(z, y, x, core):
    return (((z % 4 * 4 + y % 4) * 2 + x // 2) * 2 + core) * 2 + x % 2


CHIPS = [(z, y, x) for z in range(RING) for y in range(RING) for x in range(RING)]


def per_core(images, texts):
    return [
        (device(*chip, core), device(*to(*chip), core)) for chip in CHIPS for core, to in enumerate((images, texts))
    ]


def ring(turn):
    return per_core(lambda z, y, x: (z - turn, y, x), lambda z, y, x: (z, y - turn, x))


def reduce_pairs(turn, flip):
    return per_core(
        lambda z, y, x: (z + turn, y, x ^ flip), lambda z, y, x: (z, y + turn, 3 - x if flip else x)
    )


CORES_SWAP = [(device(*chip, core), device(*chip, 1 - core)) for chip in CHIPS for core in range(2)]
NEAR_SWAP = per_core(*[lambda z, y, x: (z, y, x ^ 1)] * 2)
FAR_SWAP = per_core(*[lambda z, y, x: (z, y, 3 - x)] * 2)
TEXTS_SWAP = per_core(lambda z, y, x: (z, y, x), lambda z, y, x: (z, y, 3 - x))

REDUCE_GROUPS = [
    [device(z, y, x, 0) for y in range(RING) for x in pair] for z in range(RING) for pair in ((0, 3), (1, 2))
] + [[device(z, y, x, 1) for z in range(RING) for x in pair] for y in range(RING) for pair in ((0, 1), (2, 3))]


def position():
    dp = lax.axis_index("dp")
    return (
        lax.div(dp, 16),
        lax.rem(lax.div(dp, 4), 4),
        lax.rem(lax.div(dp, 2), 2),
        lax.rem(dp, 2),
        lax.axis_index("tower"),
    )


def vmem():
    return pl.BlockSpec(memory_space=pltpu.VMEM)


def pick_kernel(img_feats, txt_feats, img_head, txt_head, mine, give, top, bottom, sems):
    core = position()[3]
    part = top.shape[0]

    def copies(feats, other, head):
        moves = ((other, give), (head.at[:part], top), (head.at[part:], bottom), (feats, mine))
        return [pltpu.make_async_copy(*move, sems.at[i]) for i, move in enumerate(moves)]

    @pl.when(core == 0)
    def _():
        for copy in copies(img_feats, txt_feats, img_head):
            copy.start()

    @pl.when(core == 1)
    def _():
        for copy in copies(txt_feats, img_feats, txt_head):
            copy.start()

    for copy in copies(img_feats, txt_feats, img_head):
        copy.wait()


def flip_rows(feats, flip_ref, lane):
    z, y, high, core, _ = position()
    part = flip_ref.shape[2] // RING
    turned = feats.T

    def store(own, ring_first):
        for block in range(2 * RING * RING):
            first, second, side = block // 8, block // 2 % 4, block % 2
            ring, other = (first, second) if ring_first else (second, first)
            turn = lax.rem(ring - own + RING, RING)
            flip_ref[turn, lax.rem(side + high, 2), pl.ds(other * part, part), pl.ds(lane, feats.shape[0])] = (
                turned[block * part : (block + 1) * part, :]
            )

    @pl.when(core == 0)
    def _():
        store(z, True)

    @pl.when(core == 1)
    def _():
        store(y, False)


def embed_rows(feats, head, here, emb_ref, raw_ref):
    raw = jnp.dot(feats, head, preferred_element_type=F32).astype(BF16)
    wide = raw.astype(F32)
    norm = jnp.sqrt(jnp.sum(wide * wide, axis=1, keepdims=True) + norm_eps)
    emb_ref[here, :] = (wide / norm).astype(BF16)
    raw_ref[here, :] = raw


def embed_units(head, units, emb_ref, raw_ref, flip_ref):
    rows = units[0].shape[0]
    for i in range(0, len(units), 2):
        feats = jnp.concatenate([units[i][...], units[i + 1][...]], axis=0)
        embed_rows(feats, head, pl.ds(i * rows, 2 * rows), emb_ref, raw_ref)
        flip_rows(feats, flip_ref, i * rows)


def embed_first_kernel(top, bottom, far_top, far_bottom, *refs):
    *units, emb_ref, raw_ref, flip_ref, head_ref = refs
    head_ref[...] = jnp.concatenate([top[...], bottom[...], far_top[...], far_bottom[...]], axis=0).T
    embed_units(head_ref[...], units, emb_ref, raw_ref, flip_ref)


def embed_second_kernel(head_ref, *refs):
    *units, emb_ref, raw_ref, flip_ref = refs
    embed_units(head_ref[...], units, emb_ref, raw_ref, flip_ref)


def score_kernel(emb_a, emb_b, far_a, far_b, raw_a, raw_b, grad_a, grad_b, turned_a, turned_b):
    turned_a[...] = far_a[...].T
    turned_b[...] = far_b[...].T
    rows = emb_a.shape[0] // 2

    def coef(logits):
        return (logit_scale / (1.0 + jnp.exp(-(logit_scale * logits + logit_bias)))).astype(BF16)

    for emb, raw, grad, i in ((emb_a, raw_a, grad_a, 0), (emb_a, raw_a, grad_a, 1), (emb_b, raw_b, grad_b, 0), (emb_b, raw_b, grad_b, 1)):
        here = pl.ds(i * rows, rows)
        own = emb[here, :]
        logits_a = jnp.dot(own, turned_a[...], preferred_element_type=F32)
        coef_a = coef(logits_a)
        if emb is emb_a and i == 0:
            block = rows // 2
            match = lax.broadcasted_iota(jnp.int32, (block, block), 0) == lax.broadcasted_iota(
                jnp.int32, (block, block), 1
            )
            logits = logit_scale * logits_a[:block, :block] + logit_bias
            value = logit_scale / (1.0 + jnp.exp(jnp.where(match, logits, -logits)))
            upper = jnp.concatenate(
                [jnp.where(match, -value, value).astype(BF16), coef_a[:block, block:]], axis=1
            )
            coef_a = jnp.concatenate([upper, coef_a[block:, :]], axis=0)
        logits_b = jnp.dot(own, turned_b[...], preferred_element_type=F32)
        coef_b = coef(logits_b)
        direction = jnp.dot(coef_a, far_a[...], preferred_element_type=F32) + jnp.dot(
            coef_b, far_b[...], preferred_element_type=F32
        )
        wide = raw[here, :].astype(F32)
        norm = jnp.sqrt(jnp.sum(wide * wide, axis=1, keepdims=True) + norm_eps)
        unit = wide / norm
        inner = jnp.sum(unit * direction, axis=1, keepdims=True)
        grad[here, :] = ((direction - unit * inner) / norm).astype(BF16)


def terms_kernel(turns, flip_a, flip_b, grad_a, grad_b, *pieces):
    core = position()[3]
    for k, turn in enumerate(turns):
        half, rows = flip_a.shape[2], grad_a.shape[0]
        width = grad_a.shape[1] // 2
        term = jnp.dot(
            flip_a[turn].reshape(2 * half, rows), grad_a[...], preferred_element_type=F32
        ) + jnp.dot(flip_b[turn].reshape(2 * half, rows), grad_b[...], preferred_element_type=F32)
        term = term.astype(BF16)
        straight, crossed = pieces[2 * k], pieces[2 * k + 1]
        straight[:, :width] = term[:half, :width]
        crossed[:, width:] = term[half:, :width]

        @pl.when(core == 0)
        def _():
            straight[:, width:] = term[half:, width:]
            crossed[:, :width] = term[:half, width:]

        @pl.when(core == 1)
        def _():
            straight[:, width:] = term[:half, width:]
            crossed[:, :width] = term[half:, width:]


def sum_kernel(*refs):
    _, _, high, core, tower = position()
    out_ref = refs[-1]
    total = refs[0][...].astype(F32)
    for ref in refs[1:-1]:
        total += ref[...].astype(F32)
    total = total.astype(out_ref.dtype)
    twist = jnp.where(core == 0, high, tower)
    part, width = out_ref.shape[1], out_ref.shape[2] // 2
    for j in range(RING):
        for side in range(2):
            slot = 2 * j + lax.rem(side + twist, 2)
            columns = slice(side * width, (side + 1) * width)
            out_ref[slot, :, :width] = total[2 * j * part : (2 * j + 1) * part, columns]
            out_ref[slot, :, width:] = total[(2 * j + 1) * part : (2 * j + 2) * part, columns]


def kernel_call(body, name, shapes, operands, scratch=(), flops=0, exps=0, specs=None, limit=40):
    shapes = [jax.ShapeDtypeStruct(*shape) for shape in shapes]
    touched = sum(a.size * a.dtype.itemsize for a in (*shapes, *operands))
    return pl.pallas_call(
        body,
        out_shape=shapes,
        in_specs=[vmem()] * len(operands) if specs is None else specs,
        out_specs=[vmem()] * len(shapes),
        scratch_shapes=list(scratch),
        compiler_params=pltpu.CompilerParams(vmem_limit_bytes=limit * MIB),
        cost_estimate=pl.CostEstimate(flops=flops, bytes_accessed=touched, transcendentals=exps),
        name=name,
    )(*operands)


def local(img_feats, txt_feats, img_proj, txt_proj):
    rows, depth = img_feats.shape
    width = img_proj.shape[1]
    full = 2 * width
    pair = RING * rows
    part = depth // (2 * RING * RING)

    def swap(value):
        return lax.ppermute(value, AXES, CORES_SWAP)

    mine, give, top, bottom = kernel_call(
        pick_kernel,
        "pick",
        [((rows, depth), BF16)] * 2 + [((width // 2, depth), BF16)] * 2,
        (img_feats, txt_feats, img_proj.T, txt_proj.T),
        scratch=(pltpu.SemaphoreType.DMA((4,)),),
        specs=[pl.BlockSpec(memory_space=pl.ANY)] * 4,
    )
    other = swap(give)
    _, _, high, core, tower = position()
    is_mine = (high == tower).astype(jnp.int32) == core
    straight = jnp.where(is_mine, mine, other)
    crossed = jnp.where((core == 0) & is_mine, other, jnp.where((core == 0) | is_mine, mine, other))
    crossed = lax.ppermute(crossed, AXES, TEXTS_SWAP)
    turns = (0, 1, 3, 2)
    units_a = [lax.ppermute(straight, AXES, ring(turn)) if turn else straight for turn in turns]
    far_top = lax.ppermute(top, AXES, NEAR_SWAP)
    far_bottom = lax.ppermute(bottom, AXES, FAR_SWAP)
    units_b = [lax.ppermute(crossed, AXES, ring(turn)) if turn else crossed for turn in turns]

    flips = ((RING, 2, RING * part, pair), BF16)
    block = ((pair, full), BF16)
    work = 2 * pair * depth * full
    emb_a, raw_a, flip_a, head = kernel_call(
        embed_first_kernel,
        "embed_first",
        [block, block, flips, ((depth, full), BF16)],
        (top, bottom, far_top, far_bottom, *units_a),
        flops=work,
    )
    far_a = swap(emb_a)
    emb_b, raw_b, flip_b = kernel_call(
        embed_second_kernel, "embed_second", [block, block, flips], (head, *units_b), flops=work
    )
    far_b = swap(emb_b)
    grad_a, grad_b = kernel_call(
        score_kernel,
        "score",
        [block, block],
        (emb_a, emb_b, far_a, far_b, raw_a, raw_b),
        scratch=[pltpu.VMEM((full, pair), BF16)] * 2,
        flops=16 * pair * pair * full,
        exps=4 * pair * pair,
    )

    def terms(name, turns):
        return kernel_call(
            lambda *refs: terms_kernel(turns, *refs),
            name,
            [((RING * part, full), BF16)] * (2 * len(turns)),
            (flip_a, flip_b, grad_a, grad_b),
            flops=len(turns) * work // 2,
        )

    def send(pieces, turns):
        return [
            lax.ppermute(pieces[2 * k + flip], AXES, reduce_pairs(turn, flip)) if turn or flip else pieces[0]
            for k, turn in enumerate(turns)
            for flip in range(2)
        ]

    first = send(terms("terms_first", (1, 3)), (1, 3))
    second = send(terms("terms_second", (0, 2)), (0, 2))
    (sums,) = kernel_call(
        sum_kernel, "sum_terms", [((2 * RING, part // 2, full), BF16)], (*first, *second)
    )
    swapped = lax.all_to_all(sums, AXES, 0, 0, axis_index_groups=REDUCE_GROUPS, tiled=True)
    total = jnp.sum(swapped.astype(F32), axis=0)
    is_img = position()[3] == 0
    low, high = total[:, :width], total[:, width:]
    keep = jnp.where(is_img, low, high)
    got = swap(jnp.where(is_img, high, low))
    return (jnp.where(is_img, keep, got), jnp.where(is_img, got, keep))


def solution(mesh):
    return jax.shard_map(
        local,
        mesh=mesh,
        in_specs=(P("dp", None), P("dp", None), P(None, "tower"), P(None, "tower")),
        out_specs=(P("dp", "tower"), P("dp", "tower")),
        check_vma=False,
    )
```

```python
import jax
import jax.numpy as jnp
from jax import lax
from jax.experimental import pallas as pl
from jax.experimental.pallas import tpu as pltpu
from jax.sharding import PartitionSpec as P

logit_scale = 10.0
logit_bias = -10.0
norm_eps = 1e-06
AXES = ("dp", "tower")
RING = 4
MIB = 1 << 20
F32, BF16 = jnp.float32, jnp.bfloat16


def device(z, y, x, core):
    return (((z % 4 * 4 + y % 4) * 2 + x // 2) * 2 + core) * 2 + x % 2


CHIPS = [(z, y, x) for z in range(RING) for y in range(RING) for x in range(RING)]


def block_of(x):
    return int(x // 2 == x % 2)


def per_core(images, texts):
    return [
        (device(*chip, core), device(*to(*chip), core)) for chip in CHIPS for core, to in enumerate((images, texts))
    ]


def ring(turn):
    return per_core(lambda z, y, x: (z + turn, y, x), lambda z, y, x: (z, y + turn, x))


def first_ring(turn):
    return [(device(z, y, x, 1 - block_of(x)), device(z + turn, y, x, 0)) for z, y, x in CHIPS] + [
        (device(z, y, x, block_of(x)), device(z, y + turn, x, 1)) for z, y, x in CHIPS
    ]


CORES_SWAP = [(device(*chip, core), device(*chip, 1 - core)) for chip in CHIPS for core in range(2)]
NEAR_SWAP = per_core(*[lambda z, y, x: (z, y, x ^ 1)] * 2)
FAR_SWAP = per_core(*[lambda z, y, x: (z, y, 3 - x)] * 2)
TEXTS_SWAP = [(device(z, y, x, block_of(x)), device(z, y, 3 - x, 1)) for z, y, x in CHIPS]

REDUCE_GROUPS = [[device(z, y, x, 0) for y in range(RING) for x in range(RING)] for z in range(RING)] + [
    [device(z, y, x, 1) for z in range(RING) for x in range(RING)] for y in range(RING)
]


def position():
    dp = lax.axis_index("dp")
    return (
        lax.div(dp, 16),
        lax.rem(lax.div(dp, 4), 4),
        lax.rem(lax.div(dp, 2), 2),
        lax.rem(dp, 2),
        lax.axis_index("tower"),
    )


def vmem():
    return pl.BlockSpec(memory_space=pltpu.VMEM)


def pick_kernel(img_feats, txt_feats, img_head, txt_head, mine, give, send, top, bottom, sems):
    _, _, high, core, tower = position()
    part = top.shape[0]

    def copies(feats, other, head):
        moves = ((head.at[:part], top), (head.at[part:], bottom), (other, give), (feats, mine))
        return [pltpu.make_async_copy(*move, sems.at[i]) for i, move in enumerate(moves)]

    def choice(feats):
        return pltpu.make_async_copy(feats, send, sems.at[4])

    @pl.when(core == 0)
    def _():
        for copy in copies(img_feats, txt_feats, img_head):
            copy.start()

    @pl.when(core == 1)
    def _():
        for copy in copies(txt_feats, img_feats, txt_head):
            copy.start()

    holds_block = (high == tower).astype(jnp.int32) == core

    @pl.when(holds_block)
    def _():
        choice(txt_feats).start()

    @pl.when(jnp.logical_not(holds_block))
    def _():
        choice(img_feats).start()

    for copy in copies(img_feats, txt_feats, img_head):
        copy.wait()
    choice(img_feats).wait()


def embed_units(head, units, emb_ref, raw_ref):
    rows = units[0].shape[0]
    for i in range(0, len(units), 2):
        here = pl.ds(i * rows, 2 * rows)
        feats = jnp.concatenate([units[i][...], units[i + 1][...]], axis=0)
        raw = jnp.dot(feats, head, preferred_element_type=F32).astype(BF16)
        wide = raw.astype(F32)
        norm = jnp.sqrt(jnp.sum(wide * wide, axis=1, keepdims=True) + norm_eps)
        emb_ref[here, :] = (wide / norm).astype(BF16)
        raw_ref[here, :] = raw


def embed_first_kernel(top, bottom, far_top, far_bottom, *refs):
    *units, emb_ref, raw_ref, head_ref = refs
    head_ref[...] = jnp.concatenate([top[...], bottom[...], far_top[...], far_bottom[...]], axis=0).T
    embed_units(head_ref[...], units, emb_ref, raw_ref)


def embed_second_kernel(head_ref, *refs):
    *units, emb_ref, raw_ref = refs
    embed_units(head_ref[...], units, emb_ref, raw_ref)


def flip_rows(feats, flip_ref, lane):
    z, y, _, core, _ = position()
    part = flip_ref.shape[1] // RING
    turned = feats.T

    def store(own, ring_first):
        for block in range(RING * RING):
            first, second = divmod(block, RING)
            place, other = (first, second) if ring_first else (second, first)
            turn = lax.rem(place - own + RING, RING)
            flip_ref[turn, pl.ds(other * part, part), pl.ds(lane, feats.shape[0])] = (
                turned[block * part : (block + 1) * part, :]
            )

    @pl.when(core == 0)
    def _():
        store(z, True)

    @pl.when(core == 1)
    def _():
        store(y, False)


def coefs(products):
    return (logit_scale / (1.0 + jnp.exp(-(logit_scale * products + logit_bias)))).astype(BF16)


def with_positives(products, result, here):
    block = result.shape[0] // 2
    match = lax.broadcasted_iota(jnp.int32, (block, block), 0) == lax.broadcasted_iota(
        jnp.int32, (block, block), 1
    )
    match = match & here
    logits = logit_scale * products[:block, :block] + logit_bias
    value = logit_scale / (1.0 + jnp.exp(jnp.where(match, logits, -logits)))
    upper = jnp.concatenate([jnp.where(match, -value, value).astype(BF16), result[:block, block:]], axis=1)
    return jnp.concatenate([upper, result[block:, :]], axis=0)


def score_first_kernel(*refs):
    core = position()[3]
    emb_a, emb_b, far_a = refs[:3]
    *units, coef_a, coef_b, flip_a, flip_b, turned = refs[3:]
    turned[...] = far_a[...].T
    rows = emb_a.shape[0] // 2
    for emb, coef_ref in ((emb_a, coef_a), (emb_b, coef_b)):
        for i in range(2):
            here = pl.ds(i * rows, rows)
            products = jnp.dot(emb[here, :], turned[...], preferred_element_type=F32)
            result = coefs(products)
            if emb is emb_b and i == 0:
                result = with_positives(products, result, core == 0)
            coef_ref[here, :] = result
    for i, unit in enumerate(units):
        flip_rows(unit[...], flip_a if i < RING else flip_b, i % RING * unit.shape[0])


def score_second_kernel(emb_a, emb_b, far_a, far_b, raw_a, raw_b, coef_a, coef_b, grad_a, grad_b, turned):
    core = position()[3]
    turned[...] = far_b[...].T
    rows = emb_a.shape[0] // 2
    for emb, raw, coef, grad in ((emb_a, raw_a, coef_a, grad_a), (emb_b, raw_b, coef_b, grad_b)):
        for i in range(2):
            here = pl.ds(i * rows, rows)
            products = jnp.dot(emb[here, :], turned[...], preferred_element_type=F32)
            result = coefs(products)
            if emb is emb_a and i == 0:
                result = with_positives(products, result, core == 1)
            direction = jnp.dot(coef[here, :], far_a[...], preferred_element_type=F32) + jnp.dot(
                result, far_b[...], preferred_element_type=F32
            )
            wide = raw[here, :].astype(F32)
            norm = jnp.sqrt(jnp.sum(wide * wide, axis=1, keepdims=True) + norm_eps)
            unit = wide / norm
            inner = jnp.sum(unit * direction, axis=1, keepdims=True)
            grad[here, :] = ((direction - unit * inner) / norm).astype(BF16)


def term_kernel(turn, flip_a, flip_b, grad_a, grad_b, piece):
    piece[...] = (
        jnp.dot(flip_a[turn], grad_a[...], preferred_element_type=F32)
        + jnp.dot(flip_b[turn], grad_b[...], preferred_element_type=F32)
    ).astype(piece.dtype)


def sum_kernel(*refs):
    tower = position()[4]
    out_ref = refs[-1]
    total = refs[0][...].astype(F32)
    for ref in refs[1:-1]:
        total += ref[...].astype(F32)
    total = total.astype(out_ref.dtype)
    part, width = out_ref.shape[1], out_ref.shape[2] // 2
    for j in range(2 * RING):
        for half in range(2):
            slot = 2 * j + lax.rem(half + tower, 2)
            columns = slice(half * width, (half + 1) * width)
            out_ref[slot, :, :width] = total[2 * j * part : (2 * j + 1) * part, columns]
            out_ref[slot, :, width:] = total[(2 * j + 1) * part : (2 * j + 2) * part, columns]


def kernel_call(body, name, shapes, operands, scratch=(), flops=0, exps=0, specs=None, limit=40):
    shapes = [jax.ShapeDtypeStruct(*shape) for shape in shapes]
    touched = sum(a.size * a.dtype.itemsize for a in (*shapes, *operands))
    return pl.pallas_call(
        body,
        out_shape=shapes,
        in_specs=[vmem()] * len(operands) if specs is None else specs,
        out_specs=[vmem()] * len(shapes),
        scratch_shapes=list(scratch),
        compiler_params=pltpu.CompilerParams(vmem_limit_bytes=limit * MIB),
        cost_estimate=pl.CostEstimate(flops=flops, bytes_accessed=touched, transcendentals=exps),
        name=name,
    )(*operands)


def local(img_feats, txt_feats, img_proj, txt_proj):
    rows, depth = img_feats.shape
    width = img_proj.shape[1]
    full = 2 * width
    pair = RING * rows
    part = depth // RING

    def swap(value):
        return lax.ppermute(value, AXES, CORES_SWAP)

    mine, give, send, top, bottom = kernel_call(
        pick_kernel,
        "pick",
        [((rows, depth), BF16)] * 3 + [((5 * depth // 18, depth), BF16), ((2 * depth // 9, depth), BF16)],
        (img_feats, txt_feats, img_proj.T, txt_proj.T),
        scratch=(pltpu.SemaphoreType.DMA((5,)),),
        specs=[pl.BlockSpec(memory_space=pltpu.HBM)] * 4,
        limit=60,
    )
    far_top = lax.ppermute(top, AXES, NEAR_SWAP)
    far_bottom = lax.ppermute(bottom, AXES, FAR_SWAP)
    far_texts = lax.ppermute(send, AXES, TEXTS_SWAP)
    turns = (1, 3, 2)
    units_a = [lax.ppermute(send, AXES, first_ring(turn)) for turn in turns]
    other = swap(give)
    _, _, high, core, tower = position()
    block = (high == tower).astype(jnp.int32)
    first = jnp.where(block == 1, mine, other)
    second = jnp.where(core == 1, far_texts, jnp.where(block == 0, mine, other))
    units_a = [first, *units_a]
    units_b = [second] + [lax.ppermute(second, AXES, ring(turn)) for turn in turns]

    rows_of = ((pair, full), BF16)
    work = 2 * pair * depth * full
    emb_a, raw_a, head = kernel_call(
        embed_first_kernel,
        "embed_first",
        [rows_of, rows_of, ((depth, full), BF16)],
        (top, bottom, far_top, far_bottom, *units_a),
        flops=work,
    )
    far_a = swap(emb_a)
    emb_b, raw_b = kernel_call(
        embed_second_kernel, "embed_second", [rows_of, rows_of], (head, *units_b), flops=work
    )
    far_b = swap(emb_b)
    square = ((pair, pair), BF16)
    flips = ((RING, part, pair), BF16)
    turned = pltpu.VMEM((full, pair), BF16)
    coef_a, coef_b, flip_a, flip_b = kernel_call(
        score_first_kernel,
        "score_first",
        [square, square, flips, flips],
        (emb_a, emb_b, far_a, *units_a, *units_b),
        scratch=[turned],
        flops=4 * pair * pair * full,
        exps=2 * pair * pair,
    )
    grad_a, grad_b = kernel_call(
        score_second_kernel,
        "score_second",
        [rows_of, rows_of],
        (emb_a, emb_b, far_a, far_b, raw_a, raw_b, coef_a, coef_b),
        scratch=[turned],
        flops=12 * pair * pair * full,
        exps=2 * pair * pair,
    )

    def term(turn):
        return kernel_call(
            lambda *refs: term_kernel(turn, *refs),
            "term_" + str(turn),
            [((part, full), BF16)],
            (flip_a, flip_b, grad_a, grad_b),
            flops=work // 2,
        )[0]

    sent = [lax.ppermute(term(turn), AXES, ring(turn)) for turn in (2, 1, 3)]
    (sums,) = kernel_call(
        sum_kernel, "sum_terms", [((RING * RING, part // RING // 4, full), BF16)], (term(0), *sent)
    )
    swapped = lax.all_to_all(sums, AXES, 0, 0, axis_index_groups=REDUCE_GROUPS, tiled=True)
    total = jnp.sum(swapped.astype(F32), axis=0)
    is_img = position()[3] == 0
    low, high = total[:, :width], total[:, width:]
    keep = jnp.where(is_img, low, high)
    got = swap(jnp.where(is_img, high, low))
    return (jnp.where(is_img, keep, got), jnp.where(is_img, got, keep))


def solution(mesh):
    return jax.shard_map(
        local,
        mesh=mesh,
        in_specs=(P("dp", None), P("dp", None), P(None, "tower"), P(None, "tower")),
        out_specs=(P("dp", "tower"), P("dp", "tower")),
        check_vma=False,
    )
```

```python
import jax
import jax.numpy as jnp
from jax import lax
from jax.experimental import pallas as pl
from jax.experimental.pallas import tpu as pltpu
from jax.sharding import PartitionSpec as P

logit_scale = 10.0
logit_bias = -10.0
norm_eps = 1e-06
AXES = ("dp", "tower")
RING = 4
MIB = 1 << 20
F32, BF16 = jnp.float32, jnp.bfloat16


def device(z, y, x, core):
    return (((z % 4 * 4 + y % 4) * 2 + x // 2) * 2 + core) * 2 + x % 2


CHIPS = [(z, y, x) for z in range(RING) for y in range(RING) for x in range(RING)]


def block_of(x):
    return int(x // 2 == x % 2)


def per_core(images, texts):
    return [
        (device(*chip, core), device(*to(*chip), core)) for chip in CHIPS for core, to in enumerate((images, texts))
    ]


def ring(turn):
    return per_core(lambda z, y, x: (z + turn, y, x), lambda z, y, x: (z, y + turn, x))


def first_ring(turn):
    return [(device(z, y, x, 1 - block_of(x)), device(z + turn, y, x, 0)) for z, y, x in CHIPS] + [
        (device(z, y, x, block_of(x)), device(z, y + turn, x, 1)) for z, y, x in CHIPS
    ]


CORES_SWAP = [(device(*chip, core), device(*chip, 1 - core)) for chip in CHIPS for core in range(2)]
NEAR_SWAP = per_core(*[lambda z, y, x: (z, y, x ^ 1)] * 2)
FAR_SWAP = per_core(*[lambda z, y, x: (z, y, 3 - x)] * 2)
TEXTS_SWAP = [(device(z, y, x, block_of(x)), device(z, y, 3 - x, 1)) for z, y, x in CHIPS]

REDUCE_GROUPS = [[device(z, y, x, 0) for y in range(RING) for x in range(RING)] for z in range(RING)] + [
    [device(z, y, x, 1) for z in range(RING) for x in range(RING)] for y in range(RING)
]


def position():
    dp = lax.axis_index("dp")
    return (
        lax.div(dp, 16),
        lax.rem(lax.div(dp, 4), 4),
        lax.rem(lax.div(dp, 2), 2),
        lax.rem(dp, 2),
        lax.axis_index("tower"),
    )


def pick_kernel(img_feats, txt_feats, img_head, txt_head, mine, give, send, top, bottom, sems):
    _, _, high, core, tower = position()
    split, step = top.shape[0], 64

    def copies(feats, other, head):
        moves = [(head.at[pl.ds(i, step)], top.at[pl.ds(i, step)]) for i in range(0, split, step)]
        moves += [
            (head.at[pl.ds(split + i, step)], bottom.at[pl.ds(i, step)])
            for i in range(0, bottom.shape[0], step)
        ]
        moves += [(other, give), (feats, mine)]
        return [pltpu.make_async_copy(*move, sems.at[i]) for i, move in enumerate(moves)]

    def choice(feats):
        return pltpu.make_async_copy(feats, send, sems.at[sems.shape[0] - 1])

    holds_block = (high == tower).astype(jnp.int32) == core

    @pl.when(holds_block)
    def _():
        choice(txt_feats).start()

    @pl.when(jnp.logical_not(holds_block))
    def _():
        choice(img_feats).start()

    @pl.when(core == 0)
    def _():
        for copy in copies(img_feats, txt_feats, img_head):
            copy.start()

    @pl.when(core == 1)
    def _():
        for copy in copies(txt_feats, img_feats, txt_head):
            copy.start()

    for copy in copies(img_feats, txt_feats, img_head):
        copy.wait()
    choice(img_feats).wait()


def embed_units(head, units, emb_ref, raw_ref):
    rows = units[0].shape[0]
    for i in range(0, len(units), 2):
        here = pl.ds(i * rows, 2 * rows)
        feats = jnp.concatenate([units[i][...], units[i + 1][...]], axis=0)
        raw = jnp.dot(feats, head, preferred_element_type=F32).astype(BF16)
        wide = raw.astype(F32)
        norm = jnp.sqrt(jnp.sum(wide * wide, axis=1, keepdims=True) + norm_eps)
        emb_ref[here, :] = (wide / norm).astype(BF16)
        raw_ref[here, :] = raw


def head_kernel(top, bottom, far_top, far_bottom, head_ref):
    head_ref[...] = jnp.concatenate([top[...], bottom[...], far_top[...], far_bottom[...]], axis=0).T


def embed_kernel(head_ref, *refs):
    *units, emb_ref, raw_ref = refs
    embed_units(head_ref[...], units, emb_ref, raw_ref)


def flip_rows(feats, flip_ref, lane):
    z, y, _, core, _ = position()
    part = flip_ref.shape[1] // RING
    turned = feats.T

    def store(own, ring_first):
        for block in range(RING * RING):
            first, second = divmod(block, RING)
            place, other = (first, second) if ring_first else (second, first)
            turn = lax.rem(place - own + RING, RING)
            flip_ref[turn, pl.ds(other * part, part), pl.ds(lane, feats.shape[0])] = (
                turned[block * part : (block + 1) * part, :]
            )

    @pl.when(core == 0)
    def _():
        store(z, True)

    @pl.when(core == 1)
    def _():
        store(y, False)


def coefs(products):
    return (logit_scale / (1.0 + jnp.exp(-(logit_scale * products + logit_bias)))).astype(BF16)


def with_positives(products, result, here):
    block = result.shape[0] // 2
    match = lax.broadcasted_iota(jnp.int32, (block, block), 0) == lax.broadcasted_iota(
        jnp.int32, (block, block), 1
    )
    match = match & here
    logits = logit_scale * products[:block, :block] + logit_bias
    value = logit_scale / (1.0 + jnp.exp(jnp.where(match, logits, -logits)))
    upper = jnp.concatenate([jnp.where(match, -value, value).astype(BF16), result[:block, block:]], axis=1)
    return jnp.concatenate([upper, result[block:, :]], axis=0)


def score_first_kernel(*refs):
    core = position()[3]
    emb_a, emb_b, far_a = refs[:3]
    *units, coef_a, coef_b, flip_a, flip_b, turned = refs[3:]
    turned[...] = far_a[...].T
    rows = emb_a.shape[0] // 2
    for emb, coef_ref in ((emb_a, coef_a), (emb_b, coef_b)):
        for i in range(2):
            here = pl.ds(i * rows, rows)
            products = jnp.dot(emb[here, :], turned[...], preferred_element_type=F32)
            result = coefs(products)
            if emb is emb_b and i == 0:
                result = with_positives(products, result, core == 0)
            coef_ref[here, :] = result
    for i, unit in enumerate(units):
        flip_rows(unit[...], flip_a if i < RING else flip_b, i % RING * unit.shape[0])


def score_second_kernel(emb_a, emb_b, far_a, far_b, raw_a, raw_b, coef_a, coef_b, flip_a, flip_b, grad_a, grad_b, piece, turned):
    core = position()[3]
    turned[...] = far_b[...].T
    rows = emb_a.shape[0] // 2
    for emb, raw, coef, grad in ((emb_a, raw_a, coef_a, grad_a), (emb_b, raw_b, coef_b, grad_b)):
        for i in range(2):
            here = pl.ds(i * rows, rows)
            products = jnp.dot(emb[here, :], turned[...], preferred_element_type=F32)
            result = coefs(products)
            if emb is emb_a and i == 0:
                result = with_positives(products, result, core == 1)
            direction = jnp.dot(coef[here, :], far_a[...], preferred_element_type=F32) + jnp.dot(
                result, far_b[...], preferred_element_type=F32
            )
            wide = raw[here, :].astype(F32)
            norm = jnp.sqrt(jnp.sum(wide * wide, axis=1, keepdims=True) + norm_eps)
            unit = wide / norm
            inner = jnp.sum(unit * direction, axis=1, keepdims=True)
            grad[here, :] = ((direction - unit * inner) / norm).astype(BF16)
    terms_kernel((2,), flip_a, flip_b, grad_a, grad_b, piece)


def terms_kernel(turns, flip_a, flip_b, grad_a, grad_b, *pieces):
    for turn, piece in zip(turns, pieces):
        piece[...] = (
            jnp.dot(flip_a[turn], grad_a[...], preferred_element_type=F32)
            + jnp.dot(flip_b[turn], grad_b[...], preferred_element_type=F32)
        ).astype(piece.dtype)


def add_kernel(left, right, out_ref):
    out_ref[...] = left[...].astype(F32) + right[...].astype(F32)


def sum_kernel(*refs):
    tower = position()[4]
    out_ref = refs[-1]
    total = refs[0][...].astype(F32)
    for ref in refs[1:-1]:
        total += ref[...].astype(F32)
    total = total.astype(out_ref.dtype)
    part, width = out_ref.shape[1], out_ref.shape[2] // 2
    for j in range(2 * RING):
        for half in range(2):
            slot = 2 * j + lax.rem(half + tower, 2)
            columns = slice(half * width, (half + 1) * width)
            out_ref[slot, :, :width] = total[2 * j * part : (2 * j + 1) * part, columns]
            out_ref[slot, :, width:] = total[(2 * j + 1) * part : (2 * j + 2) * part, columns]


def kernel_call(body, name, shapes, operands, scratch=(), flops=0, exps=0, anywhere=False, limit=40):
    shapes = [jax.ShapeDtypeStruct(*shape) for shape in shapes]
    space = pl.BlockSpec(memory_space=pl.ANY if anywhere else pltpu.VMEM)
    touched = sum(a.size * a.dtype.itemsize for a in (*shapes, *operands))
    return pl.pallas_call(
        body,
        out_shape=shapes,
        in_specs=[space] * len(operands),
        out_specs=[space] * len(shapes),
        scratch_shapes=list(scratch),
        compiler_params=pltpu.CompilerParams(vmem_limit_bytes=limit * MIB),
        cost_estimate=pl.CostEstimate(flops=flops, bytes_accessed=touched, transcendentals=exps),
        name=name,
    )(*operands)


def local(img_feats, txt_feats, img_proj, txt_proj):
    rows, depth = img_feats.shape
    width = img_proj.shape[1]
    full = 2 * width
    pair = RING * rows
    part = depth // RING

    def swap(value):
        return lax.ppermute(value, AXES, CORES_SWAP)

    mine, give, send, top, bottom = kernel_call(
        pick_kernel,
        "pick",
        [((rows, depth), BF16)] * 3 + [((5 * depth // 18, depth), BF16), ((2 * depth // 9, depth), BF16)],
        (img_feats, txt_feats, img_proj.T, txt_proj.T),
        scratch=(pltpu.SemaphoreType.DMA((width // 64 + 3,)),),
        anywhere=True,
        limit=54,
    )
    far_top = lax.ppermute(top, AXES, NEAR_SWAP)
    far_bottom = lax.ppermute(bottom, AXES, FAR_SWAP)
    far_texts = lax.ppermute(send, AXES, TEXTS_SWAP)
    turns = (1, 3, 2)
    units_a = [lax.ppermute(send, AXES, first_ring(turn)) for turn in turns]
    other = swap(give)
    _, _, high, core, tower = position()
    block = (high == tower).astype(jnp.int32)
    first = jnp.where(block == 1, mine, other)
    second = jnp.where(core == 1, far_texts, jnp.where(block == 0, mine, other))
    units_a = [first, *units_a]
    units_b = [second] + [lax.ppermute(second, AXES, ring(turn)) for turn in turns]

    rows_of = ((pair, full), BF16)
    work = 2 * pair * depth * full
    (head,) = kernel_call(head_kernel, "head", [((depth, full), BF16)], (top, bottom, far_top, far_bottom))
    emb_a, raw_a = kernel_call(
        embed_kernel, "embed_first", [rows_of, rows_of], (head, *units_a), flops=work
    )
    far_a = swap(emb_a)
    emb_b, raw_b = kernel_call(
        embed_kernel, "embed_second", [rows_of, rows_of], (head, *units_b), flops=work
    )
    far_b = swap(emb_b)
    square = ((pair, pair), BF16)
    flips = ((RING, part, pair), BF16)
    turned = pltpu.VMEM((full, pair), BF16)
    coef_a, coef_b, flip_a, flip_b = kernel_call(
        score_first_kernel,
        "score_first",
        [square, square, flips, flips],
        (emb_a, emb_b, far_a, *units_a, *units_b),
        scratch=[turned],
        flops=4 * pair * pair * full,
        exps=2 * pair * pair,
    )
    term = ((part, full), BF16)
    grad_a, grad_b, piece = kernel_call(
        score_second_kernel,
        "score_second",
        [rows_of, rows_of, term],
        (emb_a, emb_b, far_a, far_b, raw_a, raw_b, coef_a, coef_b, flip_a, flip_b),
        scratch=[turned],
        flops=12 * pair * pair * full + work // 2,
        exps=2 * pair * pair,
    )

    def terms(name, *turns):
        return kernel_call(
            lambda *refs: terms_kernel(turns, *refs),
            name,
            [term] * len(turns),
            (flip_a, flip_b, grad_a, grad_b),
            flops=len(turns) * work // 2,
        )

    pieces = [piece, *terms("terms_near", 1, 3)]
    sent = [lax.ppermute(piece, AXES, ring(turn)) for piece, turn in zip(pieces, (2, 1, 3))]
    (kept,) = terms("term_own", 0)
    (early,) = kernel_call(add_kernel, "add_far", [((part, full), F32)], (kept, sent[0]))
    (sums,) = kernel_call(
        sum_kernel, "sum_terms", [((RING * RING, part // RING // 4, full), BF16)], (early, *sent[1:])
    )
    swapped = lax.all_to_all(sums, AXES, 0, 0, axis_index_groups=REDUCE_GROUPS, tiled=True)
    total = jnp.sum(swapped.astype(F32), axis=0)
    is_img = position()[3] == 0
    low, high = total[:, :width], total[:, width:]
    keep = jnp.where(is_img, low, high)
    got = swap(jnp.where(is_img, high, low))
    return (jnp.where(is_img, keep, got), jnp.where(is_img, got, keep))


def solution(mesh):
    return jax.shard_map(
        local,
        mesh=mesh,
        in_specs=(P("dp", None), P("dp", None), P(None, "tower"), P(None, "tower")),
        out_specs=(P("dp", "tower"), P("dp", "tower")),
        check_vma=False,
    )
```

```python
import jax
import jax.numpy as jnp
from jax import lax
from jax.experimental import pallas as pl
from jax.experimental.pallas import tpu as pltpu
from jax.sharding import PartitionSpec as P

logit_scale = 10.0
logit_bias = -10.0
norm_eps = 1e-06
AXES = ("dp", "tower")
RING = 4
MIB = 1 << 20
F32, BF16 = jnp.float32, jnp.bfloat16


def device(z, y, x, core):
    return (((z % 4 * 4 + y % 4) * 2 + x // 2) * 2 + core) * 2 + x % 2


CHIPS = [(z, y, x) for z in range(RING) for y in range(RING) for x in range(RING)]


def block_of(x):
    return int(x // 2 == x % 2)


def per_core(images, texts):
    return [
        (device(*chip, core), device(*to(*chip), core)) for chip in CHIPS for core, to in enumerate((images, texts))
    ]


def ring(turn):
    return per_core(lambda z, y, x: (z + turn, y, x), lambda z, y, x: (z, y + turn, x))


def first_ring(turn):
    return [(device(z, y, x, 1 - block_of(x)), device(z + turn, y, x, 0)) for z, y, x in CHIPS] + [
        (device(z, y, x, block_of(x)), device(z, y + turn, x, 1)) for z, y, x in CHIPS
    ]


CORES_SWAP = [(device(*chip, core), device(*chip, 1 - core)) for chip in CHIPS for core in range(2)]
NEAR_SWAP = per_core(*[lambda z, y, x: (z, y, x ^ 1)] * 2)
FAR_SWAP = per_core(*[lambda z, y, x: (z, y, 3 - x)] * 2)
TEXTS_SWAP = [(device(z, y, x, block_of(x)), device(z, y, 3 - x, 1)) for z, y, x in CHIPS]

REDUCE_GROUPS = [[device(z, y, x, 0) for y in range(RING) for x in range(RING)] for z in range(RING)] + [
    [device(z, y, x, 1) for z in range(RING) for x in range(RING)] for y in range(RING)
]


def position():
    dp = lax.axis_index("dp")
    return (
        lax.div(dp, 16),
        lax.rem(lax.div(dp, 4), 4),
        lax.rem(lax.div(dp, 2), 2),
        lax.rem(dp, 2),
        lax.axis_index("tower"),
    )


def vmem():
    return pl.BlockSpec(memory_space=pltpu.VMEM)


def anywhere_spec():
    return pl.BlockSpec(memory_space=pl.ANY)


def pick_kernel(img_feats, txt_feats, img_head, txt_head, mine, give, send, top, bottom, sems):
    _, _, high, core, tower = position()
    split, step = top.shape[0], 64

    def copies(feats, other, head):
        moves = [(head.at[pl.ds(i, step)], top.at[pl.ds(i, step)]) for i in range(0, split, step)]
        moves += [
            (head.at[pl.ds(split + i, step)], bottom.at[pl.ds(i, step)])
            for i in range(0, bottom.shape[0], step)
        ]
        moves += [(other, give), (feats, mine)]
        return [pltpu.make_async_copy(*move, sems.at[i]) for i, move in enumerate(moves)]

    def choice(feats):
        return pltpu.make_async_copy(feats, send, sems.at[sems.shape[0] - 1])

    holds_block = (high == tower).astype(jnp.int32) == core

    @pl.when(holds_block)
    def _():
        choice(txt_feats).start()

    @pl.when(jnp.logical_not(holds_block))
    def _():
        choice(img_feats).start()

    @pl.when(core == 0)
    def _():
        for copy in copies(img_feats, txt_feats, img_head):
            copy.start()

    @pl.when(core == 1)
    def _():
        for copy in copies(txt_feats, img_feats, txt_head):
            copy.start()

    for copy in copies(img_feats, txt_feats, img_head):
        copy.wait()
    choice(img_feats).wait()


def inverse_norm(wide):
    return 1.0 / jnp.sqrt(jnp.sum(wide * wide, axis=1, keepdims=True) + norm_eps)


def embed_units(head, units, emb_ref, raw_ref):
    rows = units[0].shape[0]
    for i in range(0, len(units), 2):
        here = pl.ds(i * rows, 2 * rows)
        feats = jnp.concatenate([units[i][...], units[i + 1][...]], axis=0)
        raw = jnp.dot(feats, head, preferred_element_type=F32).astype(BF16)
        wide = raw.astype(F32)
        emb_ref[here, :] = (wide * inverse_norm(wide)).astype(BF16)
        raw_ref[here, :] = raw


def flip_kernel(*refs):
    *units, flip_ref = refs
    for i, unit in enumerate(units):
        flip_rows(unit[...], flip_ref, i * unit.shape[0])


def head_kernel(top, bottom, far_top, far_bottom, _, head_ref):
    head_ref[...] = jnp.concatenate([top[...], bottom[...], far_top[...], far_bottom[...]], axis=0).T


def embed_kernel(head_ref, *refs):
    *units, emb_ref, raw_ref = refs
    embed_units(head_ref[...], units, emb_ref, raw_ref)


def flip_rows(feats, flip_ref, lane):
    z, y, _, core, _ = position()
    part = flip_ref.shape[1] // RING
    turned = feats.T

    def store(own, ring_first):
        for block in range(RING * RING):
            first, second = divmod(block, RING)
            place, other = (first, second) if ring_first else (second, first)
            turn = lax.rem(place - own + RING, RING)
            flip_ref[turn, pl.ds(other * part, part), pl.ds(lane, feats.shape[0])] = (
                turned[block * part : (block + 1) * part, :]
            )

    @pl.when(core == 0)
    def _():
        store(z, True)

    @pl.when(core == 1)
    def _():
        store(y, False)


def coefs(products):
    return (logit_scale / (1.0 + jnp.exp(-(logit_scale * products + logit_bias)))).astype(BF16)


def with_positives(products, result, here):
    block = result.shape[0] // 2
    match = lax.broadcasted_iota(jnp.int32, (block, block), 0) == lax.broadcasted_iota(
        jnp.int32, (block, block), 1
    )
    match = match & here
    logits = logit_scale * products[:block, :block] + logit_bias
    value = logit_scale / (1.0 + jnp.exp(jnp.where(match, logits, -logits)))
    upper = jnp.concatenate([jnp.where(match, -value, value).astype(BF16), result[:block, block:]], axis=1)
    return jnp.concatenate([upper, result[block:, :]], axis=0)


def score_first_kernel(*refs):
    core = position()[3]
    emb_a, emb_b, far_a = refs[:3]
    *units, coef_a, coef_b, flip_b, turned = refs[3:]
    turned[...] = far_a[...].T
    rows = emb_a.shape[0] // 2
    for emb, coef_ref in ((emb_a, coef_a), (emb_b, coef_b)):
        for i in range(2):
            here = pl.ds(i * rows, rows)
            products = jnp.dot(emb[here, :], turned[...], preferred_element_type=F32)
            result = coefs(products)
            if emb is emb_b and i == 0:
                result = with_positives(products, result, core == 0)
            coef_ref[here, :] = result
    flip_kernel(*units, flip_b)


def score_second_kernel(emb_a, emb_b, far_a, far_b, raw_a, raw_b, coef_a, coef_b, flip_a, flip_b, grad_a, grad_b, piece, turned):
    core = position()[3]
    turned[...] = far_b[...].T
    rows = emb_a.shape[0] // 2
    for emb, raw, coef, grad in ((emb_a, raw_a, coef_a, grad_a), (emb_b, raw_b, coef_b, grad_b)):
        for i in range(2):
            here = pl.ds(i * rows, rows)
            products = jnp.dot(emb[here, :], turned[...], preferred_element_type=F32)
            result = coefs(products)
            if emb is emb_a and i == 0:
                result = with_positives(products, result, core == 1)
            direction = jnp.dot(coef[here, :], far_a[...], preferred_element_type=F32) + jnp.dot(
                result, far_b[...], preferred_element_type=F32
            )
            wide = raw[here, :].astype(F32)
            inverse = inverse_norm(wide)
            unit = wide * inverse
            inner = jnp.sum(unit * direction, axis=1, keepdims=True)
            grad[here, :] = ((direction - unit * inner) * inverse).astype(BF16)
    terms_kernel((2,), flip_a, flip_b, grad_a, grad_b, piece)


def terms_kernel(turns, flip_a, flip_b, grad_a, grad_b, *pieces):
    for turn, piece in zip(turns, pieces):
        piece[...] = (
            jnp.dot(flip_a[turn], grad_a[...], preferred_element_type=F32)
            + jnp.dot(flip_b[turn], grad_b[...], preferred_element_type=F32)
        ).astype(piece.dtype)


def add_kernel(left, right, out_ref):
    out_ref[...] = left[...].astype(F32) + right[...].astype(F32)


def sum_kernel(*refs):
    tower = position()[4]
    out_ref = refs[-1]
    total = refs[0][...].astype(F32)
    for ref in refs[1:-1]:
        total += ref[...].astype(F32)
    total = total.astype(out_ref.dtype)
    part, width = out_ref.shape[1], out_ref.shape[2] // 2
    for j in range(2 * RING):
        for half in range(2):
            slot = 2 * j + lax.rem(half + tower, 2)
            columns = slice(half * width, (half + 1) * width)
            out_ref[slot, :, :width] = total[2 * j * part : (2 * j + 1) * part, columns]
            out_ref[slot, :, width:] = total[(2 * j + 1) * part : (2 * j + 2) * part, columns]


def kernel_call(body, name, shapes, operands, scratch=(), flops=0, exps=0, anywhere=(), limit=40):
    shapes = [jax.ShapeDtypeStruct(*shape) for shape in shapes]
    touched = sum(a.size * a.dtype.itemsize for a in (*shapes, *operands))
    return pl.pallas_call(
        body,
        out_shape=shapes,
        in_specs=[anywhere_spec() if i in anywhere else vmem() for i in range(len(operands))],
        out_specs=[vmem()] * len(shapes),
        scratch_shapes=list(scratch),
        compiler_params=pltpu.CompilerParams(vmem_limit_bytes=limit * MIB),
        cost_estimate=pl.CostEstimate(flops=flops, bytes_accessed=touched, transcendentals=exps),
        name=name,
    )(*operands)


def local(img_feats, txt_feats, img_proj, txt_proj):
    rows, depth = img_feats.shape
    width = img_proj.shape[1]
    full = 2 * width
    pair = RING * rows
    part = depth // RING

    def swap(value):
        return lax.ppermute(value, AXES, CORES_SWAP)

    mine, give, send, top, bottom = kernel_call(
        pick_kernel,
        "pick",
        [((rows, depth), BF16)] * 3 + [((5 * depth // 18, depth), BF16), ((2 * depth // 9, depth), BF16)],
        (img_feats, txt_feats, img_proj.T, txt_proj.T),
        scratch=(pltpu.SemaphoreType.DMA((width // 64 + 3,)),),
        anywhere=range(4),
        limit=56,
    )
    far_top = lax.ppermute(top, AXES, NEAR_SWAP)
    far_bottom = lax.ppermute(bottom, AXES, FAR_SWAP)
    far_texts = lax.ppermute(send, AXES, TEXTS_SWAP)
    turns = (1, 3, 2)
    units_a = [lax.ppermute(send, AXES, first_ring(turn)) for turn in turns]
    other = swap(give)
    _, _, high, core, tower = position()
    block = (high == tower).astype(jnp.int32)
    first = jnp.where(block == 1, mine, other)
    second = jnp.where(core == 1, far_texts, jnp.where(block == 0, mine, other))
    units_a = [first, *units_a]
    units_b = [second] + [lax.ppermute(second, AXES, ring(turn)) for turn in turns]

    rows_of = ((pair, full), BF16)
    work = 2 * pair * depth * full
    flips = ((RING, part, pair), BF16)
    (flip_a,) = kernel_call(flip_kernel, "flip_first", [flips], units_a)
    (head,) = kernel_call(
        head_kernel, "head", [((depth, full), BF16)], (top, bottom, far_top, far_bottom, flip_a), anywhere=(4,)
    )
    emb_a, raw_a = kernel_call(
        embed_kernel, "embed_first", [rows_of, rows_of], (head, *units_a), flops=work
    )
    far_a = swap(emb_a)
    emb_b, raw_b = kernel_call(
        embed_kernel, "embed_second", [rows_of, rows_of], (head, *units_b), flops=work
    )
    far_b = swap(emb_b)
    square = ((pair, pair), BF16)
    turned = pltpu.VMEM((full, pair), BF16)
    coef_a, coef_b, flip_b = kernel_call(
        score_first_kernel,
        "score_first",
        [square, square, flips],
        (emb_a, emb_b, far_a, *units_b),
        scratch=[turned],
        flops=4 * pair * pair * full,
        exps=2 * pair * pair,
    )
    term = ((part, full), BF16)
    grad_a, grad_b, piece = kernel_call(
        score_second_kernel,
        "score_second",
        [rows_of, rows_of, term],
        (emb_a, emb_b, far_a, far_b, raw_a, raw_b, coef_a, coef_b, flip_a, flip_b),
        scratch=[turned],
        flops=12 * pair * pair * full + work // 2,
        exps=2 * pair * pair,
    )

    def terms(name, *turns):
        return kernel_call(
            lambda *refs: terms_kernel(turns, *refs),
            name,
            [term] * len(turns),
            (flip_a, flip_b, grad_a, grad_b),
            flops=len(turns) * work // 2,
        )

    pieces = [piece, *terms("terms_near", 1, 3)]
    sent = [lax.ppermute(piece, AXES, ring(turn)) for piece, turn in zip(pieces, (2, 1, 3))]
    (kept,) = terms("term_own", 0)
    (early,) = kernel_call(add_kernel, "add_far", [((part, full), F32)], (kept, sent[0]))
    (sums,) = kernel_call(
        sum_kernel, "sum_terms", [((RING * RING, part // RING // 4, full), BF16)], (early, *sent[1:])
    )
    swapped = lax.all_to_all(sums, AXES, 0, 0, axis_index_groups=REDUCE_GROUPS, tiled=True)
    total = jnp.sum(swapped.astype(F32), axis=0)
    is_img = position()[3] == 0
    low, high = total[:, :width], total[:, width:]
    keep = jnp.where(is_img, low, high)
    got = swap(jnp.where(is_img, high, low))
    return (jnp.where(is_img, keep, got), jnp.where(is_img, got, keep))


def solution(mesh):
    return jax.shard_map(
        local,
        mesh=mesh,
        in_specs=(P("dp", None), P("dp", None), P(None, "tower"), P(None, "tower")),
        out_specs=(P("dp", "tower"), P("dp", "tower")),
        check_vma=False,
    )
```

```python
import jax
import jax.numpy as jnp
from jax import lax
from jax.experimental import pallas as pl
from jax.experimental.pallas import tpu as pltpu
from jax.sharding import PartitionSpec as P

logit_scale = 10.0
logit_bias = -10.0
norm_eps = 1e-06
AXES = ("dp", "tower")
RING = 4
MIB = 1 << 20
F32, BF16 = jnp.float32, jnp.bfloat16


def device(z, y, x, core):
    return (((z % 4 * 4 + y % 4) * 2 + x // 2) * 2 + core) * 2 + x % 2


CHIPS = [(z, y, x) for z in range(RING) for y in range(RING) for x in range(RING)]


def block_of(x):
    return int(x // 2 == x % 2)


def per_core(images, texts):
    return [
        (device(*chip, core), device(*to(*chip), core)) for chip in CHIPS for core, to in enumerate((images, texts))
    ]


def ring(turn):
    return per_core(lambda z, y, x: (z + turn, y, x), lambda z, y, x: (z, y + turn, x))


def first_ring(turn):
    return [(device(z, y, x, 1 - block_of(x)), device(z + turn, y, x, 0)) for z, y, x in CHIPS] + [
        (device(z, y, x, block_of(x)), device(z, y + turn, x, 1)) for z, y, x in CHIPS
    ]


CORES_SWAP = [(device(*chip, core), device(*chip, 1 - core)) for chip in CHIPS for core in range(2)]
IMG_HEADS = [(device(z, y, x, 0), device(z, y, x ^ 1, 0)) for z, y, x in CHIPS]
TXT_HEADS = [(device(z, y, x, 1), device(z, y, 3 - x, 1)) for z, y, x in CHIPS]
TEXTS_SWAP = [(device(z, y, x, block_of(x)), device(z, y, 3 - x, 1)) for z, y, x in CHIPS]

REDUCE_GROUPS = [[device(z, y, x, 0) for y in range(RING) for x in range(RING)] for z in range(RING)] + [
    [device(z, y, x, 1) for z in range(RING) for x in range(RING)] for y in range(RING)
]


def position():
    dp = lax.axis_index("dp")
    return (
        lax.div(dp, 16),
        lax.rem(lax.div(dp, 4), 4),
        lax.rem(lax.div(dp, 2), 2),
        lax.rem(dp, 2),
        lax.axis_index("tower"),
    )


def vmem():
    return pl.BlockSpec(memory_space=pltpu.VMEM)


def inverse_norm(wide):
    return 1.0 / jnp.sqrt(jnp.sum(wide * wide, axis=1, keepdims=True) + norm_eps)


def embed_units(head, units, emb_ref, raw_ref):
    rows = units[0].shape[0]
    for i in range(0, len(units), 2):
        here = pl.ds(i * rows, 2 * rows)
        feats = jnp.concatenate([units[i][...], units[i + 1][...]], axis=0)
        raw = jnp.dot(feats, head, preferred_element_type=F32).astype(BF16)
        wide = raw.astype(F32)
        emb_ref[here, :] = (wide * inverse_norm(wide)).astype(BF16)
        raw_ref[here, :] = raw


def flip_kernel(*refs):
    *units, flip_ref = refs
    for i, unit in enumerate(units):
        flip_rows(unit[...], flip_ref, i * unit.shape[0])


def head_kernel(img_head, txt_head, far_img, far_txt, head_ref):
    core = position()[3]

    @pl.when(core == 0)
    def _():
        head_ref[...] = jnp.concatenate([img_head[...], far_img[...]], axis=0).T

    @pl.when(core == 1)
    def _():
        head_ref[...] = jnp.concatenate([txt_head[...], far_txt[...]], axis=0).T


def embed_kernel(head_ref, *refs):
    *units, emb_ref, raw_ref = refs
    embed_units(head_ref[...], units, emb_ref, raw_ref)


def flip_rows(feats, flip_ref, lane):
    z, y, _, core, _ = position()
    part = flip_ref.shape[1] // RING
    turned = feats.T

    def store(own, ring_first):
        for block in range(RING * RING):
            first, second = divmod(block, RING)
            place, other = (first, second) if ring_first else (second, first)
            turn = lax.rem(place - own + RING, RING)
            flip_ref[turn, pl.ds(other * part, part), pl.ds(lane, feats.shape[0])] = (
                turned[block * part : (block + 1) * part, :]
            )

    @pl.when(core == 0)
    def _():
        store(z, True)

    @pl.when(core == 1)
    def _():
        store(y, False)


def coefs(products):
    return (logit_scale / (1.0 + jnp.exp(-(logit_scale * products + logit_bias)))).astype(BF16)


def with_positives(products, result, here):
    block = result.shape[0] // 2
    match = lax.broadcasted_iota(jnp.int32, (block, block), 0) == lax.broadcasted_iota(
        jnp.int32, (block, block), 1
    )
    match = match & here
    logits = logit_scale * products[:block, :block] + logit_bias
    value = logit_scale / (1.0 + jnp.exp(jnp.where(match, logits, -logits)))
    upper = jnp.concatenate([jnp.where(match, -value, value).astype(BF16), result[:block, block:]], axis=1)
    return jnp.concatenate([upper, result[block:, :]], axis=0)


def score_first_kernel(*refs):
    core = position()[3]
    emb_a, emb_b, far_a = refs[:3]
    *units, coef_a, coef_b, flip_a, flip_b, turned = refs[3:]
    turned[...] = far_a[...].T
    rows = emb_a.shape[0] // 2
    for emb, coef_ref in ((emb_a, coef_a), (emb_b, coef_b)):
        for i in range(2):
            here = pl.ds(i * rows, rows)
            products = jnp.dot(emb[here, :], turned[...], preferred_element_type=F32)
            result = coefs(products)
            if emb is emb_b and i == 0:
                result = with_positives(products, result, core == 0)
            coef_ref[here, :] = result
    flip_kernel(*units[:RING], flip_a)
    flip_kernel(*units[RING:], flip_b)


def score_second_kernel(emb_a, emb_b, far_a, far_b, raw_a, raw_b, coef_a, coef_b, flip_a, flip_b, grad_a, grad_b, piece, turned):
    core = position()[3]
    turned[...] = far_b[...].T
    rows = emb_a.shape[0] // 2
    for emb, raw, coef, grad in ((emb_a, raw_a, coef_a, grad_a), (emb_b, raw_b, coef_b, grad_b)):
        for i in range(2):
            here = pl.ds(i * rows, rows)
            products = jnp.dot(emb[here, :], turned[...], preferred_element_type=F32)
            result = coefs(products)
            if emb is emb_a and i == 0:
                result = with_positives(products, result, core == 1)
            direction = jnp.dot(coef[here, :], far_a[...], preferred_element_type=F32) + jnp.dot(
                result, far_b[...], preferred_element_type=F32
            )
            wide = raw[here, :].astype(F32)
            inverse = inverse_norm(wide)
            unit = wide * inverse
            inner = jnp.sum(unit * direction, axis=1, keepdims=True)
            grad[here, :] = ((direction - unit * inner) * inverse).astype(BF16)
    terms_kernel((2,), flip_a, flip_b, grad_a, grad_b, piece)


def terms_kernel(turns, flip_a, flip_b, grad_a, grad_b, *pieces):
    for turn, piece in zip(turns, pieces):
        piece[...] = (
            jnp.dot(flip_a[turn], grad_a[...], preferred_element_type=F32)
            + jnp.dot(flip_b[turn], grad_b[...], preferred_element_type=F32)
        ).astype(piece.dtype)


def add_kernel(left, right, out_ref):
    out_ref[...] = left[...].astype(F32) + right[...].astype(F32)


def sum_kernel(*refs):
    tower = position()[4]
    out_ref = refs[-1]
    total = refs[0][...].astype(F32)
    for ref in refs[1:-1]:
        total += ref[...].astype(F32)
    total = total.astype(out_ref.dtype)
    part, width = out_ref.shape[1], out_ref.shape[2] // 2
    for j in range(2 * RING):
        for half in range(2):
            slot = 2 * j + lax.rem(half + tower, 2)
            columns = slice(half * width, (half + 1) * width)
            out_ref[slot, :, :width] = total[2 * j * part : (2 * j + 1) * part, columns]
            out_ref[slot, :, width:] = total[(2 * j + 1) * part : (2 * j + 2) * part, columns]


def kernel_call(body, name, shapes, operands, scratch=(), flops=0, exps=0, limit=40):
    shapes = [jax.ShapeDtypeStruct(*shape) for shape in shapes]
    touched = sum(a.size * a.dtype.itemsize for a in (*shapes, *operands))
    return pl.pallas_call(
        body,
        out_shape=shapes,
        in_specs=[vmem()] * len(operands),
        out_specs=[vmem()] * len(shapes),
        scratch_shapes=list(scratch),
        compiler_params=pltpu.CompilerParams(vmem_limit_bytes=limit * MIB),
        cost_estimate=pl.CostEstimate(flops=flops, bytes_accessed=touched, transcendentals=exps),
        name=name,
    )(*operands)


def local(img_feats, txt_feats, img_proj, txt_proj):
    rows, depth = img_feats.shape
    width = img_proj.shape[1]
    full = 2 * width
    pair = RING * rows
    part = depth // RING

    def swap(value):
        return lax.ppermute(value, AXES, CORES_SWAP)

    _, _, high, core, tower = position()
    block = (high == tower).astype(jnp.int32)
    is_img = core == 0
    img_head, txt_head = img_proj.T, txt_proj.T
    far_img = lax.ppermute(img_head, AXES, IMG_HEADS)
    far_txt = lax.ppermute(txt_head, AXES, TXT_HEADS)
    send = jnp.where(block == core, txt_feats, img_feats)
    far_texts = lax.ppermute(send, AXES, TEXTS_SWAP)
    turns = (1, 3, 2)
    units_a = [lax.ppermute(send, AXES, first_ring(turn)) for turn in turns]
    mine = jnp.where(is_img, img_feats, txt_feats)
    other = swap(jnp.where(is_img, txt_feats, img_feats))
    first = jnp.where(block == 1, mine, other)
    second = jnp.where(is_img, jnp.where(block == 0, mine, other), far_texts)
    units_a = [first, *units_a]
    units_b = [second] + [lax.ppermute(second, AXES, ring(turn)) for turn in turns]

    rows_of = ((pair, full), BF16)
    work = 2 * pair * depth * full
    flips = ((RING, part, pair), BF16)
    (head,) = kernel_call(
        head_kernel, "head", [((depth, full), BF16)], (img_head, txt_head, far_img, far_txt)
    )
    emb_a, raw_a = kernel_call(
        embed_kernel, "embed_first", [rows_of, rows_of], (head, *units_a), flops=work
    )
    far_a = swap(emb_a)
    emb_b, raw_b = kernel_call(
        embed_kernel, "embed_second", [rows_of, rows_of], (head, *units_b), flops=work
    )
    far_b = swap(emb_b)
    square = ((pair, pair), BF16)
    turned = pltpu.VMEM((full, pair), BF16)
    coef_a, coef_b, flip_a, flip_b = kernel_call(
        score_first_kernel,
        "score_first",
        [square, square, flips, flips],
        (emb_a, emb_b, far_a, *units_a, *units_b),
        scratch=[turned],
        flops=4 * pair * pair * full,
        exps=2 * pair * pair,
    )
    term = ((part, full), BF16)
    grad_a, grad_b, piece = kernel_call(
        score_second_kernel,
        "score_second",
        [rows_of, rows_of, term],
        (emb_a, emb_b, far_a, far_b, raw_a, raw_b, coef_a, coef_b, flip_a, flip_b),
        scratch=[turned],
        flops=12 * pair * pair * full + work // 2,
        exps=2 * pair * pair,
    )

    def terms(name, *turns):
        return kernel_call(
            lambda *refs: terms_kernel(turns, *refs),
            name,
            [term] * len(turns),
            (flip_a, flip_b, grad_a, grad_b),
            flops=len(turns) * work // 2,
        )

    pieces = [piece, *terms("terms_near", 1, 3)]
    sent = [lax.ppermute(piece, AXES, ring(turn)) for piece, turn in zip(pieces, (2, 1, 3))]
    (kept,) = terms("term_own", 0)
    (early,) = kernel_call(add_kernel, "add_far", [((part, full), F32)], (kept, sent[0]))
    (sums,) = kernel_call(
        sum_kernel, "sum_terms", [((RING * RING, part // RING // 4, full), BF16)], (early, *sent[1:])
    )
    swapped = lax.all_to_all(sums, AXES, 0, 0, axis_index_groups=REDUCE_GROUPS, tiled=True)
    total = jnp.sum(swapped.astype(F32), axis=0)
    low, high = total[:, :width], total[:, width:]
    keep = jnp.where(is_img, low, high)
    got = swap(jnp.where(is_img, high, low))
    return (jnp.where(is_img, keep, got), jnp.where(is_img, got, keep))


def solution(mesh):
    return jax.shard_map(
        local,
        mesh=mesh,
        in_specs=(P("dp", None), P("dp", None), P(None, "tower"), P(None, "tower")),
        out_specs=(P("dp", "tower"), P("dp", "tower")),
        check_vma=False,
    )
```

```python
import jax
import jax.numpy as jnp
from jax import lax
from jax.experimental import pallas as pl
from jax.experimental.pallas import tpu as pltpu
from jax.sharding import PartitionSpec as P

logit_scale = 10.0
logit_bias = -10.0
norm_eps = 1e-06
AXES = ("dp", "tower")
RING = 4
MIB = 1 << 20
F32, BF16 = jnp.float32, jnp.bfloat16


def device(z, y, x, core):
    return (((z % 4 * 4 + y % 4) * 2 + x // 2) * 2 + core) * 2 + x % 2


CHIPS = [(z, y, x) for z in range(RING) for y in range(RING) for x in range(RING)]


def block_of(x):
    return int(x // 2 == x % 2)


def per_core(images, texts):
    return [
        (device(*chip, core), device(*to(*chip), core)) for chip in CHIPS for core, to in enumerate((images, texts))
    ]


def ring(turn):
    return per_core(lambda z, y, x: (z + turn, y, x), lambda z, y, x: (z, y + turn, x))


def first_ring(turn):
    return [(device(z, y, x, 1 - block_of(x)), device(z + turn, y, x, 0)) for z, y, x in CHIPS] + [
        (device(z, y, x, block_of(x)), device(z, y + turn, x, 1)) for z, y, x in CHIPS
    ]


CORES_SWAP = [(device(*chip, core), device(*chip, 1 - core)) for chip in CHIPS for core in range(2)]
IMAGES_DOWN = [(device(*chip, 1), device(*chip, 0)) for chip in CHIPS]
TEXTS_UP = [(device(*chip, 0), device(*chip, 1)) for chip in CHIPS]
IMG_HEADS = [(device(z, y, x, 0), device(z, y, x ^ 1, 0)) for z, y, x in CHIPS]
TXT_HEADS = [(device(z, y, x, 1), device(z, y, 3 - x, 1)) for z, y, x in CHIPS]
TEXTS_SWAP = [(device(z, y, x, block_of(x)), device(z, y, 3 - x, 1)) for z, y, x in CHIPS]

REDUCE_GROUPS = [[device(z, y, x, 0) for y in range(RING) for x in range(RING)] for z in range(RING)] + [
    [device(z, y, x, 1) for z in range(RING) for x in range(RING)] for y in range(RING)
]


def position():
    dp = lax.axis_index("dp")
    return (
        lax.div(dp, 16),
        lax.rem(lax.div(dp, 4), 4),
        lax.rem(lax.div(dp, 2), 2),
        lax.rem(dp, 2),
        lax.axis_index("tower"),
    )


def vmem():
    return pl.BlockSpec(memory_space=pltpu.VMEM)


def inverse_norm(wide):
    return 1.0 / jnp.sqrt(jnp.sum(wide * wide, axis=1, keepdims=True) + norm_eps)


def embed_units(head, units, emb_ref, raw_ref):
    rows = units[0].shape[0]
    for i in range(0, len(units), 2):
        here = pl.ds(i * rows, 2 * rows)
        feats = jnp.concatenate([units[i][...], units[i + 1][...]], axis=0)
        raw = jnp.dot(feats, head, preferred_element_type=F32).astype(BF16)
        wide = raw.astype(F32)
        emb_ref[here, :] = (wide * inverse_norm(wide)).astype(BF16)
        raw_ref[here, :] = raw


def flip_kernel(*refs):
    *units, flip_ref = refs
    for i, unit in enumerate(units):
        flip_rows(unit[...], flip_ref, i * unit.shape[0])


def send_kernel(img_feats, txt_feats, send):
    _, _, high, core, tower = position()
    holds_block = (high == tower).astype(jnp.int32) == core

    @pl.when(holds_block)
    def _():
        send[...] = txt_feats[...]

    @pl.when(jnp.logical_not(holds_block))
    def _():
        send[...] = img_feats[...]


def own_kernel(img_head, txt_head, img_feats, txt_feats, other_img, other_txt, far_texts, first, second, head, sems):
    _, _, high, core, tower = position()
    block = (high == tower).astype(jnp.int32)
    step = head.shape[0] // sems.shape[0]

    def copies(source):
        return [
            pltpu.make_async_copy(source.at[pl.ds(i * step, step)], head.at[pl.ds(i * step, step)], sems.at[i])
            for i in range(sems.shape[0])
        ]

    @pl.when(core == 0)
    def _():
        for copy in copies(img_head):
            copy.start()

    @pl.when(core == 1)
    def _():
        for copy in copies(txt_head):
            copy.start()

    @pl.when((core == 0) & (block == 0))
    def _():
        first[...] = other_img[...]
        second[...] = img_feats[...]

    @pl.when((core == 0) & (block == 1))
    def _():
        first[...] = img_feats[...]
        second[...] = other_img[...]

    @pl.when(core == 1)
    def _():
        second[...] = far_texts[...]

    @pl.when((core == 1) & (block == 0))
    def _():
        first[...] = other_txt[...]

    @pl.when((core == 1) & (block == 1))
    def _():
        first[...] = txt_feats[...]

    for copy in copies(img_head):
        copy.wait()


def head_kernel(own, far_img, far_txt, head_ref):
    core = position()[3]

    @pl.when(core == 0)
    def _():
        head_ref[...] = jnp.concatenate([own[...], far_img[...]], axis=0).T

    @pl.when(core == 1)
    def _():
        head_ref[...] = jnp.concatenate([own[...], far_txt[...]], axis=0).T


def embed_kernel(head_ref, *refs):
    *units, emb_ref, raw_ref = refs
    embed_units(head_ref[...], units, emb_ref, raw_ref)


def flip_rows(feats, flip_ref, lane):
    z, y, _, core, _ = position()
    part = flip_ref.shape[1] // RING
    turned = feats.T

    def store(own, ring_first):
        for block in range(RING * RING):
            first, second = divmod(block, RING)
            place, other = (first, second) if ring_first else (second, first)
            turn = lax.rem(place - own + RING, RING)
            flip_ref[turn, pl.ds(other * part, part), pl.ds(lane, feats.shape[0])] = (
                turned[block * part : (block + 1) * part, :]
            )

    @pl.when(core == 0)
    def _():
        store(z, True)

    @pl.when(core == 1)
    def _():
        store(y, False)


def coefs(products):
    return (logit_scale / (1.0 + jnp.exp(-(logit_scale * products + logit_bias)))).astype(BF16)


def with_positives(products, result, here):
    block = result.shape[0] // 2
    match = lax.broadcasted_iota(jnp.int32, (block, block), 0) == lax.broadcasted_iota(
        jnp.int32, (block, block), 1
    )
    match = match & here
    logits = logit_scale * products[:block, :block] + logit_bias
    value = logit_scale / (1.0 + jnp.exp(jnp.where(match, logits, -logits)))
    upper = jnp.concatenate([jnp.where(match, -value, value).astype(BF16), result[:block, block:]], axis=1)
    return jnp.concatenate([upper, result[block:, :]], axis=0)


def score_first_kernel(*refs):
    core = position()[3]
    emb_a, emb_b, far_a = refs[:3]
    *units, coef_a, coef_b, flip_a, flip_b, turned = refs[3:]
    turned[...] = far_a[...].T
    rows = emb_a.shape[0] // 2
    for emb, coef_ref in ((emb_a, coef_a), (emb_b, coef_b)):
        for i in range(2):
            here = pl.ds(i * rows, rows)
            products = jnp.dot(emb[here, :], turned[...], preferred_element_type=F32)
            result = coefs(products)
            if emb is emb_b and i == 0:
                result = with_positives(products, result, core == 0)
            coef_ref[here, :] = result
    flip_kernel(*units[:RING], flip_a)
    flip_kernel(*units[RING:], flip_b)


def score_second_kernel(emb_a, emb_b, far_a, far_b, raw_a, raw_b, coef_a, coef_b, flip_a, flip_b, grad_a, grad_b, piece, turned):
    core = position()[3]
    turned[...] = far_b[...].T
    rows = emb_a.shape[0] // 2
    for emb, raw, coef, grad in ((emb_a, raw_a, coef_a, grad_a), (emb_b, raw_b, coef_b, grad_b)):
        for i in range(2):
            here = pl.ds(i * rows, rows)
            products = jnp.dot(emb[here, :], turned[...], preferred_element_type=F32)
            result = coefs(products)
            if emb is emb_a and i == 0:
                result = with_positives(products, result, core == 1)
            direction = jnp.dot(coef[here, :], far_a[...], preferred_element_type=F32) + jnp.dot(
                result, far_b[...], preferred_element_type=F32
            )
            wide = raw[here, :].astype(F32)
            inverse = inverse_norm(wide)
            unit = wide * inverse
            inner = jnp.sum(unit * direction, axis=1, keepdims=True)
            grad[here, :] = ((direction - unit * inner) * inverse).astype(BF16)
    terms_kernel((2,), flip_a, flip_b, grad_a, grad_b, piece)


def terms_kernel(turns, flip_a, flip_b, grad_a, grad_b, *pieces):
    for turn, piece in zip(turns, pieces):
        piece[...] = (
            jnp.dot(flip_a[turn], grad_a[...], preferred_element_type=F32)
            + jnp.dot(flip_b[turn], grad_b[...], preferred_element_type=F32)
        ).astype(piece.dtype)


def add_kernel(left, right, out_ref):
    out_ref[...] = left[...].astype(F32) + right[...].astype(F32)


def sum_kernel(*refs):
    tower = position()[4]
    out_ref = refs[-1]
    total = refs[0][...].astype(F32)
    for ref in refs[1:-1]:
        total += ref[...].astype(F32)
    total = total.astype(out_ref.dtype)
    part, width = out_ref.shape[1], out_ref.shape[2] // 2
    for j in range(2 * RING):
        for half in range(2):
            slot = 2 * j + lax.rem(half + tower, 2)
            columns = slice(half * width, (half + 1) * width)
            out_ref[slot, :, :width] = total[2 * j * part : (2 * j + 1) * part, columns]
            out_ref[slot, :, width:] = total[(2 * j + 1) * part : (2 * j + 2) * part, columns]


def kernel_call(body, name, shapes, operands, scratch=(), flops=0, exps=0, anywhere=0, limit=40):
    shapes = [jax.ShapeDtypeStruct(*shape) for shape in shapes]
    touched = sum(a.size * a.dtype.itemsize for a in (*shapes, *operands))
    return pl.pallas_call(
        body,
        out_shape=shapes,
        in_specs=[pl.BlockSpec(memory_space=pl.ANY)] * anywhere + [vmem()] * (len(operands) - anywhere),
        out_specs=[vmem()] * len(shapes),
        scratch_shapes=list(scratch),
        compiler_params=pltpu.CompilerParams(vmem_limit_bytes=limit * MIB),
        cost_estimate=pl.CostEstimate(flops=flops, bytes_accessed=touched, transcendentals=exps),
        name=name,
    )(*operands)


def local(img_feats, txt_feats, img_proj, txt_proj):
    rows, depth = img_feats.shape
    width = img_proj.shape[1]
    full = 2 * width
    pair = RING * rows
    part = depth // RING

    def swap(value):
        return lax.ppermute(value, AXES, CORES_SWAP)

    is_img = position()[3] == 0
    img_head, txt_head = img_proj.T, txt_proj.T
    unit = ((rows, depth), BF16)
    far_texts = lax.ppermute(txt_feats, AXES, TEXTS_SWAP)
    far_img = lax.ppermute(img_head, AXES, IMG_HEADS)
    far_txt = lax.ppermute(txt_head, AXES, TXT_HEADS)
    other_img = lax.ppermute(img_feats, AXES, IMAGES_DOWN)
    other_txt = lax.ppermute(txt_feats, AXES, TEXTS_UP)
    (send,) = kernel_call(send_kernel, "send", [unit], (img_feats, txt_feats))
    turns = (1, 3, 2)
    units_a = [lax.ppermute(send, AXES, first_ring(turn)) for turn in turns]
    first, second, own_head = kernel_call(
        own_kernel,
        "own",
        [unit, unit, ((width, depth), BF16)],
        (img_head, txt_head, img_feats, txt_feats, other_img, other_txt, far_texts),
        scratch=(pltpu.SemaphoreType.DMA((4,)),),
        anywhere=2,
    )
    units_a = [first, *units_a]
    units_b = [second] + [lax.ppermute(second, AXES, ring(turn)) for turn in turns]

    rows_of = ((pair, full), BF16)
    work = 2 * pair * depth * full
    flips = ((RING, part, pair), BF16)
    (head,) = kernel_call(
        head_kernel, "head", [((depth, full), BF16)], (own_head, far_img, far_txt)
    )
    emb_a, raw_a = kernel_call(
        embed_kernel, "embed_first", [rows_of, rows_of], (head, *units_a), flops=work
    )
    far_a = swap(emb_a)
    emb_b, raw_b = kernel_call(
        embed_kernel, "embed_second", [rows_of, rows_of], (head, *units_b), flops=work
    )
    far_b = swap(emb_b)
    square = ((pair, pair), BF16)
    turned = pltpu.VMEM((full, pair), BF16)
    coef_a, coef_b, flip_a, flip_b = kernel_call(
        score_first_kernel,
        "score_first",
        [square, square, flips, flips],
        (emb_a, emb_b, far_a, *units_a, *units_b),
        scratch=[turned],
        flops=4 * pair * pair * full,
        exps=2 * pair * pair,
    )
    term = ((part, full), BF16)
    grad_a, grad_b, piece = kernel_call(
        score_second_kernel,
        "score_second",
        [rows_of, rows_of, term],
        (emb_a, emb_b, far_a, far_b, raw_a, raw_b, coef_a, coef_b, flip_a, flip_b),
        scratch=[turned],
        flops=12 * pair * pair * full + work // 2,
        exps=2 * pair * pair,
    )

    def terms(name, *turns):
        return kernel_call(
            lambda *refs: terms_kernel(turns, *refs),
            name,
            [term] * len(turns),
            (flip_a, flip_b, grad_a, grad_b),
            flops=len(turns) * work // 2,
        )

    pieces = [piece, *terms("terms_near", 1, 3)]
    sent = [lax.ppermute(piece, AXES, ring(turn)) for piece, turn in zip(pieces, (2, 1, 3))]
    (kept,) = terms("term_own", 0)
    (early,) = kernel_call(add_kernel, "add_far", [((part, full), F32)], (kept, sent[0]))
    (sums,) = kernel_call(
        sum_kernel, "sum_terms", [((RING * RING, part // RING // 4, full), BF16)], (early, *sent[1:])
    )
    swapped = lax.all_to_all(sums, AXES, 0, 0, axis_index_groups=REDUCE_GROUPS, tiled=True)
    total = jnp.sum(swapped.astype(F32), axis=0)
    low, high = total[:, :width], total[:, width:]
    keep = jnp.where(is_img, low, high)
    got = swap(jnp.where(is_img, high, low))
    return (jnp.where(is_img, keep, got), jnp.where(is_img, got, keep))


def solution(mesh):
    return jax.shard_map(
        local,
        mesh=mesh,
        in_specs=(P("dp", None), P("dp", None), P(None, "tower"), P(None, "tower")),
        out_specs=(P("dp", "tower"), P("dp", "tower")),
        check_vma=False,
    )
```

```python
import jax
import jax.numpy as jnp
from jax import lax
from jax.experimental import pallas as pl
from jax.experimental.pallas import tpu as pltpu
from jax.sharding import PartitionSpec as P

logit_scale = 10.0
logit_bias = -10.0
norm_eps = 1e-06
AXES = ("dp", "tower")
RING = 4
MIB = 1 << 20
F32, BF16 = jnp.float32, jnp.bfloat16


def device(z, y, x, core):
    return (((z % 4 * 4 + y % 4) * 2 + x // 2) * 2 + core) * 2 + x % 2


CHIPS = [(z, y, x) for z in range(RING) for y in range(RING) for x in range(RING)]


def block_of(x):
    return int(x // 2 == x % 2)


def per_core(images, texts):
    return [
        (device(*chip, core), device(*to(*chip), core)) for chip in CHIPS for core, to in enumerate((images, texts))
    ]


def ring(turn):
    return per_core(lambda z, y, x: (z + turn, y, x), lambda z, y, x: (z, y + turn, x))


def first_ring(turn):
    return [(device(z, y, x, 1 - block_of(x)), device(z + turn, y, x, 0)) for z, y, x in CHIPS] + [
        (device(z, y, x, block_of(x)), device(z, y + turn, x, 1)) for z, y, x in CHIPS
    ]


CORES_SWAP = [(device(*chip, core), device(*chip, 1 - core)) for chip in CHIPS for core in range(2)]
NEAR_SWAP = per_core(*[lambda z, y, x: (z, y, x ^ 1)] * 2)
FAR_SWAP = per_core(*[lambda z, y, x: (z, y, 3 - x)] * 2)
TEXTS_SWAP = [(device(z, y, x, block_of(x)), device(z, y, 3 - x, 1)) for z, y, x in CHIPS]

def reduce_pairs(turn, flip):
    return per_core(
        lambda z, y, x: (z + turn, y, x ^ flip), lambda z, y, x: (z, y + turn, 3 - x if flip else x)
    )


REDUCE_GROUPS = [
    [device(z, y, x, 0) for y in range(RING) for x in pair] for z in range(RING) for pair in ((0, 3), (1, 2))
] + [[device(z, y, x, 1) for z in range(RING) for x in pair] for y in range(RING) for pair in ((0, 1), (2, 3))]


def position():
    dp = lax.axis_index("dp")
    return (
        lax.div(dp, 16),
        lax.rem(lax.div(dp, 4), 4),
        lax.rem(lax.div(dp, 2), 2),
        lax.rem(dp, 2),
        lax.axis_index("tower"),
    )


def vmem():
    return pl.BlockSpec(memory_space=pltpu.VMEM)


def anywhere_spec():
    return pl.BlockSpec(memory_space=pl.ANY)


def pick_kernel(img_feats, txt_feats, img_head, txt_head, mine, give, send, top, bottom, *scratch):
    _, _, high, core, tower = position()
    head, units, into, out = scratch
    split, step = top.shape[0], 64
    cuts = range(0, head.shape[0], step)
    count = len(cuts) + 3

    def loads(feats, other, source):
        moves = [(source.at[pl.ds(i, step)], head.at[pl.ds(i, step)]) for i in cuts]
        moves += [(other, units.at[0]), (feats, units.at[1])]
        return [pltpu.make_async_copy(*move, into.at[i]) for i, move in enumerate(moves)]

    def choice(feats):
        return pltpu.make_async_copy(feats, units.at[2], into.at[count - 1])

    @pl.when(core == 0)
    def _():
        for copy in loads(img_feats, txt_feats, img_head):
            copy.start()

    @pl.when(core == 1)
    def _():
        for copy in loads(txt_feats, img_feats, txt_head):
            copy.start()

    holds_block = (high == tower).astype(jnp.int32) == core

    @pl.when(holds_block)
    def _():
        choice(txt_feats).start()

    @pl.when(jnp.logical_not(holds_block))
    def _():
        choice(img_feats).start()

    arrivals = [*loads(img_feats, txt_feats, img_head), choice(img_feats)]
    targets = [top.at[pl.ds(i, step)] if i < split else bottom.at[pl.ds(i - split, step)] for i in cuts]
    sources = [head.at[pl.ds(i, step)] for i in cuts] + [units.at[i] for i in range(3)]
    targets += [give, mine, send]
    stores = [pltpu.make_async_copy(sources[i], targets[i], out.at[i]) for i in range(count)]
    for arrival, store in zip(arrivals, stores):
        arrival.wait()
        store.start()
    for store in stores:
        store.wait()


def inverse_norm(wide):
    return 1.0 / jnp.sqrt(jnp.sum(wide * wide, axis=1, keepdims=True) + norm_eps)


def embed_units(head, units, emb_ref, raw_ref):
    rows = units[0].shape[0]
    for i in range(0, len(units), 2):
        here = pl.ds(i * rows, 2 * rows)
        feats = jnp.concatenate([units[i][...], units[i + 1][...]], axis=0)
        raw = jnp.dot(feats, head, preferred_element_type=F32).astype(BF16)
        wide = raw.astype(F32)
        emb_ref[here, :] = (wide * inverse_norm(wide)).astype(BF16)
        raw_ref[here, :] = raw


def flip_kernel(*refs):
    *units, flip_ref = refs
    for i, unit in enumerate(units):
        flip_rows(unit[...], flip_ref, i * unit.shape[0])


def head_kernel(top, bottom, far_top, far_bottom, _, head_ref):
    head_ref[...] = jnp.concatenate([top[...], bottom[...], far_top[...], far_bottom[...]], axis=0).T


def embed_kernel(head_ref, *refs):
    *units, emb_ref, raw_ref = refs
    embed_units(head_ref[...], units, emb_ref, raw_ref)


def flip_rows(feats, flip_ref, lane):
    z, y, high, core, _ = position()
    part = flip_ref.shape[2] // RING
    turned = feats.T

    def store(own, ring_first):
        for block in range(2 * RING * RING):
            first, second, side = block // 8, block // 2 % 4, block % 2
            ring, other = (first, second) if ring_first else (second, first)
            turn = lax.rem(ring - own + RING, RING)
            flip_ref[turn, lax.rem(side + high, 2), pl.ds(other * part, part), pl.ds(lane, feats.shape[0])] = (
                turned[block * part : (block + 1) * part, :]
            )

    @pl.when(core == 0)
    def _():
        store(z, True)

    @pl.when(core == 1)
    def _():
        store(y, False)


def coefs(products):
    return (logit_scale / (1.0 + jnp.exp(-(logit_scale * products + logit_bias)))).astype(BF16)


def with_positives(products, result, here):
    block = result.shape[0] // 2
    match = lax.broadcasted_iota(jnp.int32, (block, block), 0) == lax.broadcasted_iota(
        jnp.int32, (block, block), 1
    )
    match = match & here
    logits = logit_scale * products[:block, :block] + logit_bias
    value = logit_scale / (1.0 + jnp.exp(jnp.where(match, logits, -logits)))
    upper = jnp.concatenate([jnp.where(match, -value, value).astype(BF16), result[:block, block:]], axis=1)
    return jnp.concatenate([upper, result[block:, :]], axis=0)


def score_first_kernel(*refs):
    core = position()[3]
    emb_a, emb_b, far_a = refs[:3]
    *units, coef_a, coef_b, flip_b, turned = refs[3:]
    turned[...] = far_a[...].T
    rows = emb_a.shape[0] // 2
    for emb, coef_ref in ((emb_a, coef_a), (emb_b, coef_b)):
        for i in range(2):
            here = pl.ds(i * rows, rows)
            products = jnp.dot(emb[here, :], turned[...], preferred_element_type=F32)
            result = coefs(products)
            if emb is emb_b and i == 0:
                result = with_positives(products, result, core == 0)
            coef_ref[here, :] = result
    flip_kernel(*units, flip_b)


def score_second_kernel(emb_a, emb_b, far_a, far_b, raw_a, raw_b, coef_a, coef_b, flip_a, flip_b, grad_a, grad_b, straight, crossed, turned):
    core = position()[3]
    turned[...] = far_b[...].T
    rows = emb_a.shape[0] // 2
    for emb, raw, coef, grad in ((emb_a, raw_a, coef_a, grad_a), (emb_b, raw_b, coef_b, grad_b)):
        for i in range(2):
            here = pl.ds(i * rows, rows)
            products = jnp.dot(emb[here, :], turned[...], preferred_element_type=F32)
            result = coefs(products)
            if emb is emb_a and i == 0:
                result = with_positives(products, result, core == 1)
            direction = jnp.dot(coef[here, :], far_a[...], preferred_element_type=F32) + jnp.dot(
                result, far_b[...], preferred_element_type=F32
            )
            wide = raw[here, :].astype(F32)
            inverse = inverse_norm(wide)
            unit = wide * inverse
            inner = jnp.sum(unit * direction, axis=1, keepdims=True)
            grad[here, :] = ((direction - unit * inner) * inverse).astype(BF16)
    terms_kernel((2,), flip_a, flip_b, grad_a, grad_b, straight, crossed)


def terms_kernel(turns, flip_a, flip_b, grad_a, grad_b, *pieces):
    core = position()[3]
    for k, turn in enumerate(turns):
        half, rows = flip_a.shape[2], grad_a.shape[0]
        width = grad_a.shape[1] // 2
        term = jnp.dot(
            flip_a[turn].reshape(2 * half, rows), grad_a[...], preferred_element_type=F32
        ) + jnp.dot(flip_b[turn].reshape(2 * half, rows), grad_b[...], preferred_element_type=F32)
        term = term.astype(BF16)
        straight, crossed = pieces[2 * k], pieces[2 * k + 1]
        straight[:, :width] = term[:half, :width]
        crossed[:, width:] = term[half:, :width]

        @pl.when(core == 0)
        def _():
            straight[:, width:] = term[half:, width:]
            crossed[:, :width] = term[:half, width:]

        @pl.when(core == 1)
        def _():
            straight[:, width:] = term[:half, width:]
            crossed[:, :width] = term[half:, width:]


def add_kernel(*refs):
    total = refs[0][...].astype(F32)
    for ref in refs[1:-1]:
        total += ref[...].astype(F32)
    refs[-1][...] = total


def sum_kernel(*refs):
    _, _, high, core, tower = position()
    out_ref = refs[-1]
    total = refs[0][...].astype(F32)
    for ref in refs[1:-1]:
        total += ref[...].astype(F32)
    total = total.astype(out_ref.dtype)
    twist = jnp.where(core == 0, high, tower)
    part, width = out_ref.shape[1], out_ref.shape[2] // 2
    for j in range(RING):
        for side in range(2):
            slot = 2 * j + lax.rem(side + twist, 2)
            columns = slice(side * width, (side + 1) * width)
            out_ref[slot, :, :width] = total[2 * j * part : (2 * j + 1) * part, columns]
            out_ref[slot, :, width:] = total[(2 * j + 1) * part : (2 * j + 2) * part, columns]


def kernel_call(body, name, shapes, operands, scratch=(), flops=0, exps=0, anywhere=(), anywhere_out=False, limit=40):
    shapes = [jax.ShapeDtypeStruct(*shape) for shape in shapes]
    touched = sum(a.size * a.dtype.itemsize for a in (*shapes, *operands))
    return pl.pallas_call(
        body,
        out_shape=shapes,
        in_specs=[anywhere_spec() if i in anywhere else vmem() for i in range(len(operands))],
        out_specs=[anywhere_spec() if anywhere_out else vmem()] * len(shapes),
        scratch_shapes=list(scratch),
        compiler_params=pltpu.CompilerParams(vmem_limit_bytes=limit * MIB),
        cost_estimate=pl.CostEstimate(flops=flops, bytes_accessed=touched, transcendentals=exps),
        name=name,
    )(*operands)


def local(img_feats, txt_feats, img_proj, txt_proj):
    rows, depth = img_feats.shape
    width = img_proj.shape[1]
    full = 2 * width
    pair = RING * rows
    part = depth // RING

    def swap(value):
        return lax.ppermute(value, AXES, CORES_SWAP)

    far_texts = lax.ppermute(txt_feats, AXES, TEXTS_SWAP)
    mine, give, send, top, bottom = kernel_call(
        pick_kernel,
        "pick",
        [((rows, depth), BF16)] * 3 + [((5 * depth // 18, depth), BF16), ((2 * depth // 9, depth), BF16)],
        (img_feats, txt_feats, img_proj.T, txt_proj.T),
        scratch=(
            pltpu.VMEM((width, depth), BF16),
            pltpu.VMEM((3, rows, depth), BF16),
            pltpu.SemaphoreType.DMA((width // 64 + 3,)),
            pltpu.SemaphoreType.DMA((width // 64 + 3,)),
        ),
        anywhere_out=True,
        anywhere=range(4),
        limit=56,
    )
    far_top = lax.ppermute(top, AXES, NEAR_SWAP)
    far_bottom = lax.ppermute(bottom, AXES, FAR_SWAP)
    turns = (1, 3, 2)
    units_a = [lax.ppermute(send, AXES, first_ring(turn)) for turn in turns]
    other = swap(give)
    _, _, high, core, tower = position()
    block = (high == tower).astype(jnp.int32)
    first = jnp.where(block == 1, mine, other)
    second = jnp.where(core == 1, far_texts, jnp.where(block == 0, mine, other))
    units_a = [first, *units_a]
    units_b = [second] + [lax.ppermute(second, AXES, ring(turn)) for turn in turns]

    rows_of = ((pair, full), BF16)
    work = 2 * pair * depth * full
    flips = ((RING, 2, part // 2, pair), BF16)
    (flip_a,) = kernel_call(flip_kernel, "flip_first", [flips], units_a)
    (head,) = kernel_call(
        head_kernel, "head", [((depth, full), BF16)], (top, bottom, far_top, far_bottom, flip_a), anywhere=(4,)
    )
    emb_a, raw_a = kernel_call(
        embed_kernel, "embed_first", [rows_of, rows_of], (head, *units_a), flops=work
    )
    far_a = swap(emb_a)
    emb_b, raw_b = kernel_call(
        embed_kernel, "embed_second", [rows_of, rows_of], (head, *units_b), flops=work
    )
    far_b = swap(emb_b)
    square = ((pair, pair), BF16)
    turned = pltpu.VMEM((full, pair), BF16)
    coef_a, coef_b, flip_b = kernel_call(
        score_first_kernel,
        "score_first",
        [square, square, flips],
        (emb_a, emb_b, far_a, *units_b),
        scratch=[turned],
        flops=4 * pair * pair * full,
        exps=2 * pair * pair,
    )
    term = ((part // 2, full), BF16)
    grad_a, grad_b, *far = kernel_call(
        score_second_kernel,
        "score_second",
        [rows_of, rows_of, term, term],
        (emb_a, emb_b, far_a, far_b, raw_a, raw_b, coef_a, coef_b, flip_a, flip_b),
        scratch=[turned],
        flops=12 * pair * pair * full + work // 2,
        exps=2 * pair * pair,
    )

    def terms(name, *turns):
        return kernel_call(
            lambda *refs: terms_kernel(turns, *refs),
            name,
            [term] * (2 * len(turns)),
            (flip_a, flip_b, grad_a, grad_b),
            flops=len(turns) * work // 2,
        )

    def send_pieces(pieces, *turns):
        return [
            lax.ppermute(pieces[2 * k + flip], AXES, reduce_pairs(turn, flip))
            for k, turn in enumerate(turns)
            for flip in (1, 0)
        ]

    far = send_pieces(far, 2)
    near = send_pieces(terms("terms_near", 1, 3), 1, 3)
    kept, crossed = terms("term_own", 0)
    crossed = lax.ppermute(crossed, AXES, reduce_pairs(0, 1))
    (early,) = kernel_call(add_kernel, "add_far", [((part // 2, full), F32)], (kept, *far))
    (sums,) = kernel_call(
        sum_kernel, "sum_terms", [((2 * RING, part // RING // 4, full), BF16)], (early, *near, crossed)
    )
    swapped = lax.all_to_all(sums, AXES, 0, 0, axis_index_groups=REDUCE_GROUPS, tiled=True)
    total = jnp.sum(swapped.astype(F32), axis=0)
    is_img = position()[3] == 0
    low, high = total[:, :width], total[:, width:]
    keep = jnp.where(is_img, low, high)
    got = swap(jnp.where(is_img, high, low))
    return (jnp.where(is_img, keep, got), jnp.where(is_img, got, keep))


def solution(mesh):
    return jax.shard_map(
        local,
        mesh=mesh,
        in_specs=(P("dp", None), P("dp", None), P(None, "tower"), P(None, "tower")),
        out_specs=(P("dp", "tower"), P("dp", "tower")),
        check_vma=False,
    )
```

```python
import jax
import jax.numpy as jnp
from jax import lax
from jax.experimental import pallas as pl
from jax.experimental.pallas import tpu as pltpu
from jax.sharding import PartitionSpec as P

logit_scale = 10.0
logit_bias = -10.0
norm_eps = 1e-06
AXES = ("dp", "tower")
RING = 4
MIB = 1 << 20
F32, BF16 = jnp.float32, jnp.bfloat16


def device(z, y, x, core):
    return (((z % 4 * 4 + y % 4) * 2 + x // 2) * 2 + core) * 2 + x % 2


CHIPS = [(z, y, x) for z in range(RING) for y in range(RING) for x in range(RING)]


def block_of(x):
    return int(x // 2 == x % 2)


def per_core(images, texts):
    return [
        (device(*chip, core), device(*to(*chip), core)) for chip in CHIPS for core, to in enumerate((images, texts))
    ]


def ring(turn):
    return per_core(lambda z, y, x: (z + turn, y, x), lambda z, y, x: (z, y + turn, x))


def first_ring(turn):
    return [(device(z, y, x, 1 - block_of(x)), device(z + turn, y, x, 0)) for z, y, x in CHIPS] + [
        (device(z, y, x, block_of(x)), device(z, y + turn, x, 1)) for z, y, x in CHIPS
    ]


CORES_SWAP = [(device(*chip, core), device(*chip, 1 - core)) for chip in CHIPS for core in range(2)]
NEAR_SWAP = per_core(*[lambda z, y, x: (z, y, x ^ 1)] * 2)
FAR_SWAP = per_core(*[lambda z, y, x: (z, y, 3 - x)] * 2)
TEXTS_SWAP = [(device(z, y, x, block_of(x)), device(z, y, 3 - x, 1)) for z, y, x in CHIPS]

def reduce_pairs(turn, flip):
    return per_core(
        lambda z, y, x: (z + turn, y, x ^ flip), lambda z, y, x: (z, y + turn, 3 - x if flip else x)
    )


REDUCE_GROUPS = [
    [device(z, y, x, 0) for y in range(RING) for x in pair] for z in range(RING) for pair in ((0, 3), (1, 2))
] + [[device(z, y, x, 1) for z in range(RING) for x in pair] for y in range(RING) for pair in ((0, 1), (2, 3))]


def position():
    dp = lax.axis_index("dp")
    return (
        lax.div(dp, 16),
        lax.rem(lax.div(dp, 4), 4),
        lax.rem(lax.div(dp, 2), 2),
        lax.rem(dp, 2),
        lax.axis_index("tower"),
    )


def vmem():
    return pl.BlockSpec(memory_space=pltpu.VMEM)


def anywhere_spec():
    return pl.BlockSpec(memory_space=pl.ANY)


def pick_kernel(img_feats, txt_feats, img_head, txt_head, mine, give, send, top, bottom, *scratch):
    _, _, high, core, tower = position()
    head, units, into, out = scratch
    split, step = top.shape[0], 32
    cuts = range(0, head.shape[0], step)
    count = len(cuts) + 3

    def loads(feats, other, source):
        moves = [(source.at[pl.ds(i, step)], head.at[pl.ds(i, step)]) for i in cuts]
        moves += [(other, units.at[0]), (feats, units.at[1])]
        return [pltpu.make_async_copy(*move, into.at[i]) for i, move in enumerate(moves)]

    def choice(feats):
        return pltpu.make_async_copy(feats, units.at[2], into.at[count - 1])

    @pl.when(core == 0)
    def _():
        for copy in loads(img_feats, txt_feats, img_head):
            copy.start()

    @pl.when(core == 1)
    def _():
        for copy in loads(txt_feats, img_feats, txt_head):
            copy.start()

    holds_block = (high == tower).astype(jnp.int32) == core

    @pl.when(holds_block)
    def _():
        choice(txt_feats).start()

    @pl.when(jnp.logical_not(holds_block))
    def _():
        choice(img_feats).start()

    arrivals = [*loads(img_feats, txt_feats, img_head), choice(img_feats)]
    targets = [top.at[pl.ds(i, step)] if i < split else bottom.at[pl.ds(i - split, step)] for i in cuts]
    sources = [head.at[pl.ds(i, step)] for i in cuts] + [units.at[i] for i in range(3)]
    targets += [give, mine, send]
    stores = [pltpu.make_async_copy(sources[i], targets[i], out.at[i]) for i in range(count)]
    for arrival, store in zip(arrivals, stores):
        arrival.wait()
        store.start()
    for store in stores:
        store.wait()


def inverse_norm(wide):
    return 1.0 / jnp.sqrt(jnp.sum(wide * wide, axis=1, keepdims=True) + norm_eps)


def embed_units(head, units, emb_ref, raw_ref):
    rows = units[0].shape[0]
    for i in range(0, len(units), 2):
        here = pl.ds(i * rows, 2 * rows)
        feats = jnp.concatenate([units[i][...], units[i + 1][...]], axis=0)
        raw = jnp.dot(feats, head, preferred_element_type=F32).astype(BF16)
        wide = raw.astype(F32)
        emb_ref[here, :] = (wide * inverse_norm(wide)).astype(BF16)
        raw_ref[here, :] = raw


def flip_kernel(*refs):
    *units, flip_ref = refs
    for i, unit in enumerate(units):
        flip_rows(unit[...], flip_ref, i * unit.shape[0])


def own_half_kernel(top, bottom, *refs):
    *units, flip_ref, turned_ref, raw_ref = refs
    turned_ref[...] = jnp.concatenate([top[...], bottom[...]], axis=0).T
    flip_kernel(*units, flip_ref)
    rows = units[0].shape[0]
    for i in range(0, len(units), 2):
        feats = jnp.concatenate([units[i][...], units[i + 1][...]], axis=0)
        raw_ref[pl.ds(i * rows, 2 * rows), :] = jnp.dot(
            feats, turned_ref[...], preferred_element_type=F32
        ).astype(BF16)


def embed_first_kernel(turned, own_raw, far_top, far_bottom, *refs):
    *units, emb_ref, raw_ref, head_ref = refs
    width = turned.shape[1]
    far = jnp.concatenate([far_top[...], far_bottom[...]], axis=0).T
    rows = units[0].shape[0]
    for i in range(0, len(units), 2):
        here = pl.ds(i * rows, 2 * rows)
        feats = jnp.concatenate([units[i][...], units[i + 1][...]], axis=0)
        far_raw = jnp.dot(feats, far, preferred_element_type=F32).astype(BF16)
        raw = jnp.concatenate([own_raw[here, :], far_raw], axis=1)
        wide = raw.astype(F32)
        emb_ref[here, :] = (wide * inverse_norm(wide)).astype(BF16)
        raw_ref[here, :] = raw
    head_ref[:, :width] = turned[...]
    head_ref[:, width:] = far


def embed_kernel(head_ref, *refs):
    *units, emb_ref, raw_ref = refs
    embed_units(head_ref[...], units, emb_ref, raw_ref)


def flip_rows(feats, flip_ref, lane):
    z, y, high, core, _ = position()
    part = flip_ref.shape[2] // RING
    turned = feats.T

    def store(own, ring_first):
        for block in range(2 * RING * RING):
            first, second, side = block // 8, block // 2 % 4, block % 2
            ring, other = (first, second) if ring_first else (second, first)
            turn = lax.rem(ring - own + RING, RING)
            flip_ref[turn, lax.rem(side + high, 2), pl.ds(other * part, part), pl.ds(lane, feats.shape[0])] = (
                turned[block * part : (block + 1) * part, :]
            )

    @pl.when(core == 0)
    def _():
        store(z, True)

    @pl.when(core == 1)
    def _():
        store(y, False)


def coefs(products):
    return (logit_scale / (1.0 + jnp.exp(-(logit_scale * products + logit_bias)))).astype(BF16)


def with_positives(products, result, here):
    block = result.shape[0] // 2
    match = lax.broadcasted_iota(jnp.int32, (block, block), 0) == lax.broadcasted_iota(
        jnp.int32, (block, block), 1
    )
    match = match & here
    logits = logit_scale * products[:block, :block] + logit_bias
    value = logit_scale / (1.0 + jnp.exp(jnp.where(match, logits, -logits)))
    upper = jnp.concatenate([jnp.where(match, -value, value).astype(BF16), result[:block, block:]], axis=1)
    return jnp.concatenate([upper, result[block:, :]], axis=0)


def score_first_kernel(*refs):
    core = position()[3]
    emb_a, emb_b, far_a = refs[:3]
    *units, coef_a, coef_b, flip_b, turned = refs[3:]
    turned[...] = far_a[...].T
    rows = emb_a.shape[0] // 2
    for emb, coef_ref in ((emb_a, coef_a), (emb_b, coef_b)):
        for i in range(2):
            here = pl.ds(i * rows, rows)
            products = jnp.dot(emb[here, :], turned[...], preferred_element_type=F32)
            result = coefs(products)
            if emb is emb_b and i == 0:
                result = with_positives(products, result, core == 0)
            coef_ref[here, :] = result
    flip_kernel(*units, flip_b)


def score_second_kernel(emb_a, emb_b, far_a, far_b, raw_a, raw_b, coef_a, coef_b, flip_a, flip_b, grad_a, grad_b, straight, crossed, turned):
    core = position()[3]
    turned[...] = far_b[...].T
    rows = emb_a.shape[0] // 2
    for emb, raw, coef, grad in ((emb_a, raw_a, coef_a, grad_a), (emb_b, raw_b, coef_b, grad_b)):
        for i in range(2):
            here = pl.ds(i * rows, rows)
            products = jnp.dot(emb[here, :], turned[...], preferred_element_type=F32)
            result = coefs(products)
            if emb is emb_a and i == 0:
                result = with_positives(products, result, core == 1)
            direction = jnp.dot(coef[here, :], far_a[...], preferred_element_type=F32) + jnp.dot(
                result, far_b[...], preferred_element_type=F32
            )
            wide = raw[here, :].astype(F32)
            inverse = inverse_norm(wide)
            unit = wide * inverse
            inner = jnp.sum(unit * direction, axis=1, keepdims=True)
            grad[here, :] = ((direction - unit * inner) * inverse).astype(BF16)
    terms_kernel((2,), flip_a, flip_b, grad_a, grad_b, straight, crossed)


def terms_kernel(turns, flip_a, flip_b, grad_a, grad_b, *pieces):
    core = position()[3]
    for k, turn in enumerate(turns):
        half, rows = flip_a.shape[2], grad_a.shape[0]
        width = grad_a.shape[1] // 2
        term = jnp.dot(
            flip_a[turn].reshape(2 * half, rows), grad_a[...], preferred_element_type=F32
        ) + jnp.dot(flip_b[turn].reshape(2 * half, rows), grad_b[...], preferred_element_type=F32)
        term = term.astype(BF16)
        straight, crossed = pieces[2 * k], pieces[2 * k + 1]
        straight[:, :width] = term[:half, :width]
        crossed[:, width:] = term[half:, :width]

        @pl.when(core == 0)
        def _():
            straight[:, width:] = term[half:, width:]
            crossed[:, :width] = term[:half, width:]

        @pl.when(core == 1)
        def _():
            straight[:, width:] = term[:half, width:]
            crossed[:, :width] = term[half:, width:]


def add_kernel(*refs):
    total = refs[0][...].astype(F32)
    for ref in refs[1:-1]:
        total += ref[...].astype(F32)
    refs[-1][...] = total


def sum_kernel(*refs):
    _, _, high, core, tower = position()
    out_ref = refs[-1]
    total = refs[0][...].astype(F32)
    for ref in refs[1:-1]:
        total += ref[...].astype(F32)
    total = total.astype(out_ref.dtype)
    twist = jnp.where(core == 0, high, tower)
    part, width = out_ref.shape[1], out_ref.shape[2] // 2
    for j in range(RING):
        for side in range(2):
            slot = 2 * j + lax.rem(side + twist, 2)
            columns = slice(side * width, (side + 1) * width)
            out_ref[slot, :, :width] = total[2 * j * part : (2 * j + 1) * part, columns]
            out_ref[slot, :, width:] = total[(2 * j + 1) * part : (2 * j + 2) * part, columns]


def kernel_call(body, name, shapes, operands, scratch=(), flops=0, exps=0, anywhere=(), anywhere_out=False, limit=40):
    shapes = [jax.ShapeDtypeStruct(*shape) for shape in shapes]
    touched = sum(a.size * a.dtype.itemsize for a in (*shapes, *operands))
    return pl.pallas_call(
        body,
        out_shape=shapes,
        in_specs=[anywhere_spec() if i in anywhere else vmem() for i in range(len(operands))],
        out_specs=[anywhere_spec() if anywhere_out else vmem()] * len(shapes),
        scratch_shapes=list(scratch),
        compiler_params=pltpu.CompilerParams(vmem_limit_bytes=limit * MIB),
        cost_estimate=pl.CostEstimate(flops=flops, bytes_accessed=touched, transcendentals=exps),
        name=name,
    )(*operands)


def local(img_feats, txt_feats, img_proj, txt_proj):
    rows, depth = img_feats.shape
    width = img_proj.shape[1]
    full = 2 * width
    pair = RING * rows
    part = depth // RING

    def swap(value):
        return lax.ppermute(value, AXES, CORES_SWAP)

    far_texts = lax.ppermute(txt_feats, AXES, TEXTS_SWAP)
    mine, give, send, top, bottom = kernel_call(
        pick_kernel,
        "pick",
        [((rows, depth), BF16)] * 3 + [((22 * depth // 72, depth), BF16), ((14 * depth // 72, depth), BF16)],
        (img_feats, txt_feats, img_proj.T, txt_proj.T),
        scratch=(
            pltpu.VMEM((width, depth), BF16),
            pltpu.VMEM((3, rows, depth), BF16),
            pltpu.SemaphoreType.DMA((width // 32 + 3,)),
            pltpu.SemaphoreType.DMA((width // 32 + 3,)),
        ),
        anywhere_out=True,
        anywhere=range(4),
        limit=56,
    )
    far_top = lax.ppermute(top, AXES, NEAR_SWAP)
    far_bottom = lax.ppermute(bottom, AXES, FAR_SWAP)
    turns = (1, 3, 2)
    units_a = [lax.ppermute(send, AXES, first_ring(turn)) for turn in turns]
    other = swap(give)
    _, _, high, core, tower = position()
    block = (high == tower).astype(jnp.int32)
    first = jnp.where(block == 1, mine, other)
    second = jnp.where(core == 1, far_texts, jnp.where(block == 0, mine, other))
    units_a = [first, *units_a]
    units_b = [second] + [lax.ppermute(second, AXES, ring(turn)) for turn in turns]

    rows_of = ((pair, full), BF16)
    work = 2 * pair * depth * full
    flips = ((RING, 2, part // 2, pair), BF16)
    flip_a, turned_head, own_raw = kernel_call(
        own_half_kernel,
        "own_half",
        [flips, ((depth, width), BF16), ((pair, width), BF16)],
        (top, bottom, *units_a),
        flops=work // 2,
    )
    emb_a, raw_a, head = kernel_call(
        embed_first_kernel,
        "embed_first",
        [rows_of, rows_of, ((depth, full), BF16)],
        (turned_head, own_raw, far_top, far_bottom, *units_a),
        flops=work // 2,
    )
    far_a = swap(emb_a)
    emb_b, raw_b = kernel_call(
        embed_kernel, "embed_second", [rows_of, rows_of], (head, *units_b), flops=work
    )
    far_b = swap(emb_b)
    square = ((pair, pair), BF16)
    turned = pltpu.VMEM((full, pair), BF16)
    coef_a, coef_b, flip_b = kernel_call(
        score_first_kernel,
        "score_first",
        [square, square, flips],
        (emb_a, emb_b, far_a, *units_b),
        scratch=[turned],
        flops=4 * pair * pair * full,
        exps=2 * pair * pair,
    )
    term = ((part // 2, full), BF16)
    grad_a, grad_b, *far = kernel_call(
        score_second_kernel,
        "score_second",
        [rows_of, rows_of, term, term],
        (emb_a, emb_b, far_a, far_b, raw_a, raw_b, coef_a, coef_b, flip_a, flip_b),
        scratch=[turned],
        flops=12 * pair * pair * full + work // 2,
        exps=2 * pair * pair,
    )

    def terms(name, *turns):
        return kernel_call(
            lambda *refs: terms_kernel(turns, *refs),
            name,
            [term] * (2 * len(turns)),
            (flip_a, flip_b, grad_a, grad_b),
            flops=len(turns) * work // 2,
        )

    def send_pieces(pieces, *turns):
        return [
            lax.ppermute(pieces[2 * k + flip], AXES, reduce_pairs(turn, flip))
            for k, turn in enumerate(turns)
            for flip in (1, 0)
        ]

    far = send_pieces(far, 2)
    near = send_pieces(terms("term_up", 1), 1) + send_pieces(terms("term_down", 3), 3)
    kept, crossed = terms("term_own", 0)
    crossed = lax.ppermute(crossed, AXES, reduce_pairs(0, 1))
    (early,) = kernel_call(add_kernel, "add_far", [((part // 2, full), F32)], (kept, *far))
    (sums,) = kernel_call(
        sum_kernel, "sum_terms", [((2 * RING, part // RING // 4, full), BF16)], (early, *near, crossed)
    )
    swapped = lax.all_to_all(sums, AXES, 0, 0, axis_index_groups=REDUCE_GROUPS, tiled=True)
    total = jnp.sum(swapped.astype(F32), axis=0)
    is_img = position()[3] == 0
    low, high = total[:, :width], total[:, width:]
    keep = jnp.where(is_img, low, high)
    got = swap(jnp.where(is_img, high, low))
    return (jnp.where(is_img, keep, got), jnp.where(is_img, got, keep))


def solution(mesh):
    return jax.shard_map(
        local,
        mesh=mesh,
        in_specs=(P("dp", None), P("dp", None), P(None, "tower"), P(None, "tower")),
        out_specs=(P("dp", "tower"), P("dp", "tower")),
        check_vma=False,
    )
```

```python
import jax
import jax.numpy as jnp
from jax import lax
from jax.experimental import pallas as pl
from jax.experimental.pallas import tpu as pltpu
from jax.sharding import PartitionSpec as P

logit_scale = 10.0
logit_bias = -10.0
norm_eps = 1e-06
AXES = ("dp", "tower")
RING = 4
MIB = 1 << 20
F32, BF16 = jnp.float32, jnp.bfloat16


def device(z, y, x, core):
    return (((z % 4 * 4 + y % 4) * 2 + x // 2) * 2 + core) * 2 + x % 2


CHIPS = [(z, y, x) for z in range(RING) for y in range(RING) for x in range(RING)]


def block_of(x):
    return int(x // 2 == x % 2)


def per_core(images, texts):
    return [
        (device(*chip, core), device(*to(*chip), core)) for chip in CHIPS for core, to in enumerate((images, texts))
    ]


def ring(turn):
    return per_core(lambda z, y, x: (z + turn, y, x), lambda z, y, x: (z, y + turn, x))


def first_ring(turn):
    return [(device(z, y, x, 1 - block_of(x)), device(z + turn, y, x, 0)) for z, y, x in CHIPS] + [
        (device(z, y, x, block_of(x)), device(z, y + turn, x, 1)) for z, y, x in CHIPS
    ]


CORES_SWAP = [(device(*chip, core), device(*chip, 1 - core)) for chip in CHIPS for core in range(2)]
NEAR_SWAP = per_core(*[lambda z, y, x: (z, y, x ^ 1)] * 2)
FAR_SWAP = per_core(*[lambda z, y, x: (z, y, 3 - x)] * 2)
TEXTS_SWAP = [(device(z, y, x, block_of(x)), device(z, y, 3 - x, 1)) for z, y, x in CHIPS]

def reduce_pairs(turn, flip):
    return per_core(
        lambda z, y, x: (z + turn, y, x ^ flip), lambda z, y, x: (z, y + turn, 3 - x if flip else x)
    )


REDUCE_GROUPS = [
    [device(z, y, x, 0) for y in range(RING) for x in pair] for z in range(RING) for pair in ((0, 3), (1, 2))
] + [[device(z, y, x, 1) for z in range(RING) for x in pair] for y in range(RING) for pair in ((0, 1), (2, 3))]


def position():
    dp = lax.axis_index("dp")
    return (
        lax.div(dp, 16),
        lax.rem(lax.div(dp, 4), 4),
        lax.rem(lax.div(dp, 2), 2),
        lax.rem(dp, 2),
        lax.axis_index("tower"),
    )


def vmem():
    return pl.BlockSpec(memory_space=pltpu.VMEM)


def anywhere_spec():
    return pl.BlockSpec(memory_space=pl.ANY)


def pick_kernel(img_feats, txt_feats, img_head, txt_head, mine, give, send, top, bottom, *scratch):
    _, _, high, core, tower = position()
    head, units, into, out = scratch
    split = top.shape[0]
    cuts = ((0, split // 2), (split // 2, split // 2), (split, bottom.shape[0]))
    count = len(cuts) + 3

    def loads(feats, other, source):
        moves = [(source.at[pl.ds(*cut)], head.at[pl.ds(*cut)]) for cut in cuts]
        moves += [(other, units.at[0]), (feats, units.at[1])]
        return [pltpu.make_async_copy(*move, into.at[i]) for i, move in enumerate(moves)]

    def choice(feats):
        return pltpu.make_async_copy(feats, units.at[2], into.at[count - 1])

    @pl.when(core == 0)
    def _():
        for copy in loads(img_feats, txt_feats, img_head):
            copy.start()

    @pl.when(core == 1)
    def _():
        for copy in loads(txt_feats, img_feats, txt_head):
            copy.start()

    holds_block = (high == tower).astype(jnp.int32) == core

    @pl.when(holds_block)
    def _():
        choice(txt_feats).start()

    @pl.when(jnp.logical_not(holds_block))
    def _():
        choice(img_feats).start()

    arrivals = [*loads(img_feats, txt_feats, img_head), choice(img_feats)]
    targets = [top.at[pl.ds(i, n)] if i < split else bottom.at[pl.ds(i - split, n)] for i, n in cuts]
    sources = [head.at[pl.ds(*cut)] for cut in cuts] + [units.at[i] for i in range(3)]
    targets += [give, mine, send]
    stores = [pltpu.make_async_copy(sources[i], targets[i], out.at[i]) for i in range(count)]
    for arrival, store in zip(arrivals, stores):
        arrival.wait()
        store.start()
    for store in stores:
        store.wait()


def inverse_norm(wide):
    return 1.0 / jnp.sqrt(jnp.sum(wide * wide, axis=1, keepdims=True) + norm_eps)


def embed_units(head, units, emb_ref, raw_ref):
    rows = units[0].shape[0]
    for i in range(0, len(units), 2):
        here = pl.ds(i * rows, 2 * rows)
        feats = jnp.concatenate([units[i][...], units[i + 1][...]], axis=0)
        raw = jnp.dot(feats, head, preferred_element_type=F32).astype(BF16)
        wide = raw.astype(F32)
        emb_ref[here, :] = (wide * inverse_norm(wide)).astype(BF16)
        raw_ref[here, :] = raw


def flip_kernel(*refs):
    *units, flip_ref = refs
    for i, unit in enumerate(units):
        flip_rows(unit[...], flip_ref, i * unit.shape[0])


def own_half_kernel(top, bottom, *refs):
    *units, flip_ref, turned_ref, raw_ref = refs
    turned_ref[...] = jnp.concatenate([top[...], bottom[...]], axis=0).T
    flip_kernel(*units, flip_ref)
    rows = units[0].shape[0]
    for i in range(0, len(units), 2):
        feats = jnp.concatenate([units[i][...], units[i + 1][...]], axis=0)
        raw_ref[pl.ds(i * rows, 2 * rows), :] = jnp.dot(
            feats, turned_ref[...], preferred_element_type=F32
        ).astype(BF16)


def embed_first_kernel(turned, own_raw, far_top, far_bottom, *refs):
    *units, emb_ref, raw_ref, head_ref = refs
    width = turned.shape[1]
    far = jnp.concatenate([far_top[...], far_bottom[...]], axis=0).T
    rows = units[0].shape[0]
    for i in range(0, len(units), 2):
        here = pl.ds(i * rows, 2 * rows)
        feats = jnp.concatenate([units[i][...], units[i + 1][...]], axis=0)
        far_raw = jnp.dot(feats, far, preferred_element_type=F32).astype(BF16)
        raw = jnp.concatenate([own_raw[here, :], far_raw], axis=1)
        wide = raw.astype(F32)
        emb_ref[here, :] = (wide * inverse_norm(wide)).astype(BF16)
        raw_ref[here, :] = raw
    head_ref[:, :width] = turned[...]
    head_ref[:, width:] = far


def embed_kernel(head_ref, *refs):
    *units, emb_ref, raw_ref = refs
    embed_units(head_ref[...], units, emb_ref, raw_ref)


def flip_rows(feats, flip_ref, lane):
    z, y, high, core, _ = position()
    part = flip_ref.shape[2] // RING
    turned = feats.T

    def store(own, ring_first):
        for block in range(2 * RING * RING):
            first, second, side = block // 8, block // 2 % 4, block % 2
            ring, other = (first, second) if ring_first else (second, first)
            turn = lax.rem(ring - own + RING, RING)
            flip_ref[turn, lax.rem(side + high, 2), pl.ds(other * part, part), pl.ds(lane, feats.shape[0])] = (
                turned[block * part : (block + 1) * part, :]
            )

    @pl.when(core == 0)
    def _():
        store(z, True)

    @pl.when(core == 1)
    def _():
        store(y, False)


def coefs(products):
    return (logit_scale / (1.0 + jnp.exp(-(logit_scale * products + logit_bias)))).astype(BF16)


def with_positives(products, result, here):
    block = result.shape[0] // 2
    match = lax.broadcasted_iota(jnp.int32, (block, block), 0) == lax.broadcasted_iota(
        jnp.int32, (block, block), 1
    )
    match = match & here
    logits = logit_scale * products[:block, :block] + logit_bias
    value = logit_scale / (1.0 + jnp.exp(jnp.where(match, logits, -logits)))
    upper = jnp.concatenate([jnp.where(match, -value, value).astype(BF16), result[:block, block:]], axis=1)
    return jnp.concatenate([upper, result[block:, :]], axis=0)


def score_first_kernel(*refs):
    core = position()[3]
    emb_a, emb_b, far_a = refs[:3]
    *units, coef_a, coef_b, flip_b, turned = refs[3:]
    turned[...] = far_a[...].T
    rows = emb_a.shape[0] // 2
    for emb, coef_ref in ((emb_a, coef_a), (emb_b, coef_b)):
        for i in range(2):
            here = pl.ds(i * rows, rows)
            products = jnp.dot(emb[here, :], turned[...], preferred_element_type=F32)
            result = coefs(products)
            if emb is emb_b and i == 0:
                result = with_positives(products, result, core == 0)
            coef_ref[here, :] = result
    flip_kernel(*units, flip_b)


def score_second_kernel(emb_a, emb_b, far_a, far_b, raw_a, raw_b, coef_a, coef_b, flip_a, flip_b, grad_a, grad_b, straight, crossed, turned):
    core = position()[3]
    turned[...] = far_b[...].T
    rows = emb_a.shape[0] // 2
    for emb, raw, coef, grad in ((emb_a, raw_a, coef_a, grad_a), (emb_b, raw_b, coef_b, grad_b)):
        for i in range(2):
            here = pl.ds(i * rows, rows)
            products = jnp.dot(emb[here, :], turned[...], preferred_element_type=F32)
            result = coefs(products)
            if emb is emb_a and i == 0:
                result = with_positives(products, result, core == 1)
            direction = jnp.dot(coef[here, :], far_a[...], preferred_element_type=F32) + jnp.dot(
                result, far_b[...], preferred_element_type=F32
            )
            wide = raw[here, :].astype(F32)
            inverse = inverse_norm(wide)
            unit = wide * inverse
            inner = jnp.sum(unit * direction, axis=1, keepdims=True)
            grad[here, :] = ((direction - unit * inner) * inverse).astype(BF16)
    terms_kernel((2,), flip_a, flip_b, grad_a, grad_b, straight, crossed)


def terms_kernel(turns, flip_a, flip_b, grad_a, grad_b, *pieces):
    core = position()[3]
    for k, turn in enumerate(turns):
        half, rows = flip_a.shape[2], grad_a.shape[0]
        width = grad_a.shape[1] // 2
        term = jnp.dot(
            flip_a[turn].reshape(2 * half, rows), grad_a[...], preferred_element_type=F32
        ) + jnp.dot(flip_b[turn].reshape(2 * half, rows), grad_b[...], preferred_element_type=F32)
        term = term.astype(BF16)
        straight, crossed = pieces[2 * k], pieces[2 * k + 1]
        straight[:, :width] = term[:half, :width]
        crossed[:, width:] = term[half:, :width]

        @pl.when(core == 0)
        def _():
            straight[:, width:] = term[half:, width:]
            crossed[:, :width] = term[:half, width:]

        @pl.when(core == 1)
        def _():
            straight[:, width:] = term[:half, width:]
            crossed[:, :width] = term[half:, width:]


def add_kernel(*refs):
    total = refs[0][...].astype(F32)
    for ref in refs[1:-1]:
        total += ref[...].astype(F32)
    refs[-1][...] = total


def sum_kernel(*refs):
    _, _, high, core, tower = position()
    out_ref = refs[-1]
    total = refs[0][...].astype(F32)
    for ref in refs[1:-1]:
        total += ref[...].astype(F32)
    total = total.astype(out_ref.dtype)
    twist = jnp.where(core == 0, high, tower)
    part, width = out_ref.shape[1], out_ref.shape[2] // 2
    for j in range(RING):
        for side in range(2):
            slot = 2 * j + lax.rem(side + twist, 2)
            columns = slice(side * width, (side + 1) * width)
            out_ref[slot, :, :width] = total[2 * j * part : (2 * j + 1) * part, columns]
            out_ref[slot, :, width:] = total[(2 * j + 1) * part : (2 * j + 2) * part, columns]


def kernel_call(body, name, shapes, operands, scratch=(), flops=0, exps=0, anywhere=(), anywhere_out=False, limit=40):
    shapes = [jax.ShapeDtypeStruct(*shape) for shape in shapes]
    touched = sum(a.size * a.dtype.itemsize for a in (*shapes, *operands))
    return pl.pallas_call(
        body,
        out_shape=shapes,
        in_specs=[anywhere_spec() if i in anywhere else vmem() for i in range(len(operands))],
        out_specs=[anywhere_spec() if anywhere_out else vmem()] * len(shapes),
        scratch_shapes=list(scratch),
        compiler_params=pltpu.CompilerParams(vmem_limit_bytes=limit * MIB),
        cost_estimate=pl.CostEstimate(flops=flops, bytes_accessed=touched, transcendentals=exps),
        name=name,
    )(*operands)


def local(img_feats, txt_feats, img_proj, txt_proj):
    rows, depth = img_feats.shape
    width = img_proj.shape[1]
    full = 2 * width
    pair = RING * rows
    part = depth // RING

    def swap(value):
        return lax.ppermute(value, AXES, CORES_SWAP)

    far_texts = lax.ppermute(txt_feats, AXES, TEXTS_SWAP)
    mine, give, send, top, bottom = kernel_call(
        pick_kernel,
        "pick",
        [((rows, depth), BF16)] * 3 + [((22 * depth // 72, depth), BF16), ((14 * depth // 72, depth), BF16)],
        (img_feats, txt_feats, img_proj.T, txt_proj.T),
        scratch=(
            pltpu.VMEM((width, depth), BF16),
            pltpu.VMEM((3, rows, depth), BF16),
            pltpu.SemaphoreType.DMA((6,)),
            pltpu.SemaphoreType.DMA((6,)),
        ),
        anywhere_out=True,
        anywhere=range(4),
        limit=56,
    )
    far_top = lax.ppermute(top, AXES, NEAR_SWAP)
    far_bottom = lax.ppermute(bottom, AXES, FAR_SWAP)
    turns = (1, 3, 2)
    units_a = [lax.ppermute(send, AXES, first_ring(turn)) for turn in turns]
    other = swap(give)
    _, _, high, core, tower = position()
    block = (high == tower).astype(jnp.int32)
    first = jnp.where(block == 1, mine, other)
    second = jnp.where(core == 1, far_texts, jnp.where(block == 0, mine, other))
    units_a = [first, *units_a]
    units_b = [second] + [lax.ppermute(second, AXES, ring(turn)) for turn in turns]

    rows_of = ((pair, full), BF16)
    work = 2 * pair * depth * full
    flips = ((RING, 2, part // 2, pair), BF16)
    flip_a, turned_head, own_raw = kernel_call(
        own_half_kernel,
        "own_half",
        [flips, ((depth, width), BF16), ((pair, width), BF16)],
        (top, bottom, *units_a),
        flops=work // 2,
    )
    emb_a, raw_a, head = kernel_call(
        embed_first_kernel,
        "embed_first",
        [rows_of, rows_of, ((depth, full), BF16)],
        (turned_head, own_raw, far_top, far_bottom, *units_a),
        flops=work // 2,
    )
    far_a = swap(emb_a)
    emb_b, raw_b = kernel_call(
        embed_kernel, "embed_second", [rows_of, rows_of], (head, *units_b), flops=work
    )
    far_b = swap(emb_b)
    square = ((pair, pair), BF16)
    turned = pltpu.VMEM((full, pair), BF16)
    coef_a, coef_b, flip_b = kernel_call(
        score_first_kernel,
        "score_first",
        [square, square, flips],
        (emb_a, emb_b, far_a, *units_b),
        scratch=[turned],
        flops=4 * pair * pair * full,
        exps=2 * pair * pair,
    )
    term = ((part // 2, full), BF16)
    grad_a, grad_b, *far = kernel_call(
        score_second_kernel,
        "score_second",
        [rows_of, rows_of, term, term],
        (emb_a, emb_b, far_a, far_b, raw_a, raw_b, coef_a, coef_b, flip_a, flip_b),
        scratch=[turned],
        flops=12 * pair * pair * full + work // 2,
        exps=2 * pair * pair,
    )

    def terms(name, *turns):
        return kernel_call(
            lambda *refs: terms_kernel(turns, *refs),
            name,
            [term] * (2 * len(turns)),
            (flip_a, flip_b, grad_a, grad_b),
            flops=len(turns) * work // 2,
        )

    def send_pieces(pieces, *turns):
        return [
            lax.ppermute(pieces[2 * k + flip], AXES, reduce_pairs(turn, flip))
            for k, turn in enumerate(turns)
            for flip in (1, 0)
        ]

    far = send_pieces(far, 2)
    near = send_pieces(terms("term_up", 1), 1) + send_pieces(terms("term_down", 3), 3)
    kept, crossed = terms("term_own", 0)
    crossed = lax.ppermute(crossed, AXES, reduce_pairs(0, 1))
    (early,) = kernel_call(add_kernel, "add_far", [((part // 2, full), F32)], (kept, *far))
    (sums,) = kernel_call(
        sum_kernel, "sum_terms", [((2 * RING, part // RING // 4, full), BF16)], (early, *near, crossed)
    )
    swapped = lax.all_to_all(sums, AXES, 0, 0, axis_index_groups=REDUCE_GROUPS, tiled=True)
    total = jnp.sum(swapped.astype(F32), axis=0)
    is_img = position()[3] == 0
    low, high = total[:, :width], total[:, width:]
    keep = jnp.where(is_img, low, high)
    got = swap(jnp.where(is_img, high, low))
    return (jnp.where(is_img, keep, got), jnp.where(is_img, got, keep))


def solution(mesh):
    return jax.shard_map(
        local,
        mesh=mesh,
        in_specs=(P("dp", None), P("dp", None), P(None, "tower"), P(None, "tower")),
        out_specs=(P("dp", "tower"), P("dp", "tower")),
        check_vma=False,
    )
```

```python
import jax
import jax.numpy as jnp
from jax import lax
from jax.experimental import pallas as pl
from jax.experimental.pallas import tpu as pltpu
from jax.sharding import PartitionSpec as P

logit_scale = 10.0
logit_bias = -10.0
norm_eps = 1e-06
AXES = ("dp", "tower")
RING = 4
MIB = 1 << 20
F32, BF16 = jnp.float32, jnp.bfloat16


def device(z, y, x, core):
    return (((z % 4 * 4 + y % 4) * 2 + x // 2) * 2 + core) * 2 + x % 2


CHIPS = [(z, y, x) for z in range(RING) for y in range(RING) for x in range(RING)]


def block_of(x):
    return int(x // 2 == x % 2)


def per_core(images, texts):
    return [
        (device(*chip, core), device(*to(*chip), core)) for chip in CHIPS for core, to in enumerate((images, texts))
    ]


def ring(turn):
    return per_core(lambda z, y, x: (z + turn, y, x), lambda z, y, x: (z, y + turn, x))


def first_ring(turn):
    return [(device(z, y, x, 1 - block_of(x)), device(z + turn, y, x, 0)) for z, y, x in CHIPS] + [
        (device(z, y, x, block_of(x)), device(z, y + turn, x, 1)) for z, y, x in CHIPS
    ]


CORES_SWAP = [(device(*chip, core), device(*chip, 1 - core)) for chip in CHIPS for core in range(2)]
NEAR_SWAP = per_core(*[lambda z, y, x: (z, y, x ^ 1)] * 2)
FAR_SWAP = per_core(*[lambda z, y, x: (z, y, 3 - x)] * 2)
TEXTS_SWAP = [(device(z, y, x, block_of(x)), device(z, y, 3 - x, 1)) for z, y, x in CHIPS]

def reduce_pairs(turn, flip):
    return per_core(
        lambda z, y, x: (z + turn, y, x ^ flip), lambda z, y, x: (z, y + turn, 3 - x if flip else x)
    )


REDUCE_GROUPS = [
    [device(z, y, x, 0) for y in range(RING) for x in pair] for z in range(RING) for pair in ((0, 3), (1, 2))
] + [[device(z, y, x, 1) for z in range(RING) for x in pair] for y in range(RING) for pair in ((0, 1), (2, 3))]


def position():
    dp = lax.axis_index("dp")
    return (
        lax.div(dp, 16),
        lax.rem(lax.div(dp, 4), 4),
        lax.rem(lax.div(dp, 2), 2),
        lax.rem(dp, 2),
        lax.axis_index("tower"),
    )


def vmem():
    return pl.BlockSpec(memory_space=pltpu.VMEM)


def anywhere_spec():
    return pl.BlockSpec(memory_space=pl.ANY)


def pick_kernel(img_feats, txt_feats, img_head, txt_head, give, send, top, bottom, *scratch):
    _, _, high, core, tower = position()
    head, units, into, out = scratch
    split = top.shape[0]
    cuts = ((0, split // 2), (split // 2, split // 2), (split, bottom.shape[0]))
    count = len(cuts) + 2

    def loads(other, source):
        moves = [(source.at[pl.ds(*cut)], head.at[pl.ds(*cut)]) for cut in cuts]
        moves += [(other, units.at[0])]
        return [pltpu.make_async_copy(*move, into.at[i]) for i, move in enumerate(moves)]

    def choice(feats):
        return pltpu.make_async_copy(feats, units.at[1], into.at[count - 1])

    @pl.when(core == 0)
    def _():
        for copy in loads(txt_feats, img_head):
            copy.start()

    @pl.when(core == 1)
    def _():
        for copy in loads(img_feats, txt_head):
            copy.start()

    holds_block = (high == tower).astype(jnp.int32) == core

    @pl.when(holds_block)
    def _():
        choice(txt_feats).start()

    @pl.when(jnp.logical_not(holds_block))
    def _():
        choice(img_feats).start()

    arrivals = [*loads(txt_feats, img_head), choice(img_feats)]
    targets = [top.at[pl.ds(i, n)] if i < split else bottom.at[pl.ds(i - split, n)] for i, n in cuts]
    sources = [head.at[pl.ds(*cut)] for cut in cuts] + [units.at[i] for i in range(2)]
    targets += [give, send]
    stores = [pltpu.make_async_copy(sources[i], targets[i], out.at[i]) for i in range(count)]
    for arrival, store in zip(arrivals, stores):
        arrival.wait()
        store.start()
    for store in stores:
        store.wait()


def inverse_norm(wide):
    return 1.0 / jnp.sqrt(jnp.sum(wide * wide, axis=1, keepdims=True) + norm_eps)


def embed_units(head, units, emb_ref, raw_ref):
    rows = units[0].shape[0]
    for i in range(0, len(units), 2):
        here = pl.ds(i * rows, 2 * rows)
        feats = jnp.concatenate([units[i][...], units[i + 1][...]], axis=0)
        raw = jnp.dot(feats, head, preferred_element_type=F32).astype(BF16)
        wide = raw.astype(F32)
        emb_ref[here, :] = (wide * inverse_norm(wide)).astype(BF16)
        raw_ref[here, :] = raw


def flip_kernel(*refs):
    *units, flip_ref = refs
    for i, unit in enumerate(units):
        flip_rows(unit[...], flip_ref, i * unit.shape[0])


def own_half_kernel(top, bottom, *refs):
    *units, flip_ref, turned_ref, raw_ref = refs
    turned_ref[...] = jnp.concatenate([top[...], bottom[...]], axis=0).T
    flip_kernel(*units, flip_ref)
    rows = units[0].shape[0]
    for i in range(0, len(units), 2):
        feats = jnp.concatenate([units[i][...], units[i + 1][...]], axis=0)
        raw_ref[pl.ds(i * rows, 2 * rows), :] = jnp.dot(
            feats, turned_ref[...], preferred_element_type=F32
        ).astype(BF16)


def embed_first_kernel(turned, own_raw, far_top, far_bottom, *refs):
    *units, emb_ref, raw_ref, head_ref = refs
    width = turned.shape[1]
    far = jnp.concatenate([far_top[...], far_bottom[...]], axis=0).T
    rows = units[0].shape[0]
    for i in range(0, len(units), 2):
        here = pl.ds(i * rows, 2 * rows)
        feats = jnp.concatenate([units[i][...], units[i + 1][...]], axis=0)
        far_raw = jnp.dot(feats, far, preferred_element_type=F32).astype(BF16)
        raw = jnp.concatenate([own_raw[here, :], far_raw], axis=1)
        wide = raw.astype(F32)
        emb_ref[here, :] = (wide * inverse_norm(wide)).astype(BF16)
        raw_ref[here, :] = raw
    head_ref[:, :width] = turned[...]
    head_ref[:, width:] = far


def embed_kernel(head_ref, *refs):
    *units, emb_ref, raw_ref = refs
    embed_units(head_ref[...], units, emb_ref, raw_ref)


def flip_rows(feats, flip_ref, lane):
    z, y, high, core, _ = position()
    part = flip_ref.shape[2] // RING
    turned = feats.T

    def store(own, ring_first):
        for block in range(2 * RING * RING):
            first, second, side = block // 8, block // 2 % 4, block % 2
            ring, other = (first, second) if ring_first else (second, first)
            turn = lax.rem(ring - own + RING, RING)
            flip_ref[turn, lax.rem(side + high, 2), pl.ds(other * part, part), pl.ds(lane, feats.shape[0])] = (
                turned[block * part : (block + 1) * part, :]
            )

    @pl.when(core == 0)
    def _():
        store(z, True)

    @pl.when(core == 1)
    def _():
        store(y, False)


def coefs(products):
    return (logit_scale / (1.0 + jnp.exp(-(logit_scale * products + logit_bias)))).astype(BF16)


def with_positives(products, result, here):
    block = result.shape[0] // 2
    match = lax.broadcasted_iota(jnp.int32, (block, block), 0) == lax.broadcasted_iota(
        jnp.int32, (block, block), 1
    )
    match = match & here
    logits = logit_scale * products[:block, :block] + logit_bias
    value = logit_scale / (1.0 + jnp.exp(jnp.where(match, logits, -logits)))
    upper = jnp.concatenate([jnp.where(match, -value, value).astype(BF16), result[:block, block:]], axis=1)
    return jnp.concatenate([upper, result[block:, :]], axis=0)


def score_first_kernel(*refs):
    core = position()[3]
    emb_a, emb_b, far_a = refs[:3]
    *units, coef_a, coef_b, flip_b, turned = refs[3:]
    turned[...] = far_a[...].T
    rows = emb_a.shape[0] // 2
    for emb, coef_ref in ((emb_a, coef_a), (emb_b, coef_b)):
        for i in range(2):
            here = pl.ds(i * rows, rows)
            products = jnp.dot(emb[here, :], turned[...], preferred_element_type=F32)
            result = coefs(products)
            if emb is emb_b and i == 0:
                result = with_positives(products, result, core == 0)
            coef_ref[here, :] = result
    flip_kernel(*units, flip_b)


def score_second_kernel(emb_a, emb_b, far_a, far_b, raw_a, raw_b, coef_a, coef_b, flip_a, flip_b, grad_a, grad_b, straight, crossed, turned):
    core = position()[3]
    turned[...] = far_b[...].T
    rows = emb_a.shape[0] // 2
    for emb, raw, coef, grad in ((emb_a, raw_a, coef_a, grad_a), (emb_b, raw_b, coef_b, grad_b)):
        for i in range(2):
            here = pl.ds(i * rows, rows)
            products = jnp.dot(emb[here, :], turned[...], preferred_element_type=F32)
            result = coefs(products)
            if emb is emb_a and i == 0:
                result = with_positives(products, result, core == 1)
            direction = jnp.dot(coef[here, :], far_a[...], preferred_element_type=F32) + jnp.dot(
                result, far_b[...], preferred_element_type=F32
            )
            wide = raw[here, :].astype(F32)
            inverse = inverse_norm(wide)
            unit = wide * inverse
            inner = jnp.sum(unit * direction, axis=1, keepdims=True)
            grad[here, :] = ((direction - unit * inner) * inverse).astype(BF16)
    terms_kernel((2,), flip_a, flip_b, grad_a, grad_b, straight, crossed)


def terms_kernel(turns, flip_a, flip_b, grad_a, grad_b, *pieces):
    core = position()[3]
    for k, turn in enumerate(turns):
        half, rows = flip_a.shape[2], grad_a.shape[0]
        width = grad_a.shape[1] // 2
        term = jnp.dot(
            flip_a[turn].reshape(2 * half, rows), grad_a[...], preferred_element_type=F32
        ) + jnp.dot(flip_b[turn].reshape(2 * half, rows), grad_b[...], preferred_element_type=F32)
        term = term.astype(BF16)
        straight, crossed = pieces[2 * k], pieces[2 * k + 1]
        straight[:, :width] = term[:half, :width]
        crossed[:, width:] = term[half:, :width]

        @pl.when(core == 0)
        def _():
            straight[:, width:] = term[half:, width:]
            crossed[:, :width] = term[:half, width:]

        @pl.when(core == 1)
        def _():
            straight[:, width:] = term[:half, width:]
            crossed[:, :width] = term[half:, width:]


def add_kernel(*refs):
    total = refs[0][...].astype(F32)
    for ref in refs[1:-1]:
        total += ref[...].astype(F32)
    refs[-1][...] = total


def sum_kernel(*refs):
    _, _, high, core, tower = position()
    out_ref = refs[-1]
    total = refs[0][...].astype(F32)
    for ref in refs[1:-1]:
        total += ref[...].astype(F32)
    total = total.astype(out_ref.dtype)
    twist = jnp.where(core == 0, high, tower)
    part, width = out_ref.shape[1], out_ref.shape[2] // 2
    for j in range(RING):
        for side in range(2):
            slot = 2 * j + lax.rem(side + twist, 2)
            columns = slice(side * width, (side + 1) * width)
            out_ref[slot, :, :width] = total[2 * j * part : (2 * j + 1) * part, columns]
            out_ref[slot, :, width:] = total[(2 * j + 1) * part : (2 * j + 2) * part, columns]


def kernel_call(body, name, shapes, operands, scratch=(), flops=0, exps=0, anywhere=(), anywhere_out=False, limit=40):
    shapes = [jax.ShapeDtypeStruct(*shape) for shape in shapes]
    touched = sum(a.size * a.dtype.itemsize for a in (*shapes, *operands))
    return pl.pallas_call(
        body,
        out_shape=shapes,
        in_specs=[anywhere_spec() if i in anywhere else vmem() for i in range(len(operands))],
        out_specs=[anywhere_spec() if anywhere_out else vmem()] * len(shapes),
        scratch_shapes=list(scratch),
        compiler_params=pltpu.CompilerParams(vmem_limit_bytes=limit * MIB),
        cost_estimate=pl.CostEstimate(flops=flops, bytes_accessed=touched, transcendentals=exps),
        name=name,
    )(*operands)


def local(img_feats, txt_feats, img_proj, txt_proj):
    rows, depth = img_feats.shape
    width = img_proj.shape[1]
    full = 2 * width
    pair = RING * rows
    part = depth // RING

    def swap(value):
        return lax.ppermute(value, AXES, CORES_SWAP)

    far_texts = lax.ppermute(txt_feats, AXES, TEXTS_SWAP)
    give, send, top, bottom = kernel_call(
        pick_kernel,
        "pick",
        [((rows, depth), BF16)] * 2 + [((22 * depth // 72, depth), BF16), ((14 * depth // 72, depth), BF16)],
        (img_feats, txt_feats, img_proj.T, txt_proj.T),
        scratch=(
            pltpu.VMEM((width, depth), BF16),
            pltpu.VMEM((2, rows, depth), BF16),
            pltpu.SemaphoreType.DMA((5,)),
            pltpu.SemaphoreType.DMA((5,)),
        ),
        anywhere_out=True,
        anywhere=range(4),
        limit=56,
    )
    far_top = lax.ppermute(top, AXES, NEAR_SWAP)
    far_bottom = lax.ppermute(bottom, AXES, FAR_SWAP)
    turns = (1, 3, 2)
    units_a = [lax.ppermute(send, AXES, first_ring(turn)) for turn in turns]
    other = swap(give)
    mine = jnp.where(position()[3] == 0, img_feats, txt_feats)
    _, _, high, core, tower = position()
    block = (high == tower).astype(jnp.int32)
    first = jnp.where(block == 1, mine, other)
    second = jnp.where(core == 1, far_texts, jnp.where(block == 0, mine, other))
    units_a = [first, *units_a]
    units_b = [second] + [lax.ppermute(second, AXES, ring(turn)) for turn in turns]

    rows_of = ((pair, full), BF16)
    work = 2 * pair * depth * full
    flips = ((RING, 2, part // 2, pair), BF16)
    flip_a, turned_head, own_raw = kernel_call(
        own_half_kernel,
        "own_half",
        [flips, ((depth, width), BF16), ((pair, width), BF16)],
        (top, bottom, *units_a),
        flops=work // 2,
    )
    emb_a, raw_a, head = kernel_call(
        embed_first_kernel,
        "embed_first",
        [rows_of, rows_of, ((depth, full), BF16)],
        (turned_head, own_raw, far_top, far_bottom, *units_a),
        flops=work // 2,
    )
    far_a = swap(emb_a)
    emb_b, raw_b = kernel_call(
        embed_kernel, "embed_second", [rows_of, rows_of], (head, *units_b), flops=work
    )
    far_b = swap(emb_b)
    square = ((pair, pair), BF16)
    turned = pltpu.VMEM((full, pair), BF16)
    coef_a, coef_b, flip_b = kernel_call(
        score_first_kernel,
        "score_first",
        [square, square, flips],
        (emb_a, emb_b, far_a, *units_b),
        scratch=[turned],
        flops=4 * pair * pair * full,
        exps=2 * pair * pair,
    )
    term = ((part // 2, full), BF16)
    grad_a, grad_b, *far = kernel_call(
        score_second_kernel,
        "score_second",
        [rows_of, rows_of, term, term],
        (emb_a, emb_b, far_a, far_b, raw_a, raw_b, coef_a, coef_b, flip_a, flip_b),
        scratch=[turned],
        flops=12 * pair * pair * full + work // 2,
        exps=2 * pair * pair,
    )

    def terms(name, *turns):
        return kernel_call(
            lambda *refs: terms_kernel(turns, *refs),
            name,
            [term] * (2 * len(turns)),
            (flip_a, flip_b, grad_a, grad_b),
            flops=len(turns) * work // 2,
        )

    def send_pieces(pieces, *turns):
        return [
            lax.ppermute(pieces[2 * k + flip], AXES, reduce_pairs(turn, flip))
            for k, turn in enumerate(turns)
            for flip in (1, 0)
        ]

    far = send_pieces(far, 2)
    near = send_pieces(terms("term_up", 1), 1) + send_pieces(terms("term_down", 3), 3)
    kept, crossed = terms("term_own", 0)
    crossed = lax.ppermute(crossed, AXES, reduce_pairs(0, 1))
    (early,) = kernel_call(add_kernel, "add_far", [((part // 2, full), F32)], (kept, *far))
    (sums,) = kernel_call(
        sum_kernel, "sum_terms", [((2 * RING, part // RING // 4, full), BF16)], (early, *near, crossed)
    )
    swapped = lax.all_to_all(sums, AXES, 0, 0, axis_index_groups=REDUCE_GROUPS, tiled=True)
    total = jnp.sum(swapped.astype(F32), axis=0)
    is_img = position()[3] == 0
    low, high = total[:, :width], total[:, width:]
    keep = jnp.where(is_img, low, high)
    got = swap(jnp.where(is_img, high, low))
    return (jnp.where(is_img, keep, got), jnp.where(is_img, got, keep))


def solution(mesh):
    return jax.shard_map(
        local,
        mesh=mesh,
        in_specs=(P("dp", None), P("dp", None), P(None, "tower"), P(None, "tower")),
        out_specs=(P("dp", "tower"), P("dp", "tower")),
        check_vma=False,
    )
```
